256 devices in a mesh: leaf: 64 (over z, x, core), rep: 4 (over y).
Axes of the slice: x: 4, y: 4, z: 8, core: 2. Of those that a mesh axis runs over, the one named last changes fastest.
Arguments:
- points: bfloat16 [300, 262144], P(None, 'leaf'), may hold values from -0.375 to 0.375
- right_sides: bfloat16 [64, 262144], P('rep', 'leaf'), may hold values from -6 to 6
- skel_dev: int32 [64, 256], P('leaf'), may hold values from 0 to 4095, as said below
- proj_dev: bfloat16 [64, 256, 4096], P('leaf'), may hold values from -0.25 to 0.25
- skel_sel: int32 [64, 5, 256], P('leaf'), may hold values from 0 to 511, as said below
- proj_up: bfloat16 [64, 5, 256, 512], P('leaf'), as said below
- fetch_leaf: int32 [64, 64], P('leaf'), may hold values from 0 to 15
- pair_target: int32 [64, 4, 192], P('leaf', 'rep'), may hold values from 0 to 15, as said below
- pair_source: int32 [64, 4, 192], P('leaf', 'rep'), may hold values from 0 to 79, as said below
- pair_count: int32 [64, 4], P('leaf', 'rep'), may hold values from 1 to 192, as said below
- far_use: int32 [6, 1024], P(None, 'leaf'), may hold values 0 or 1
Outputs:
- matvec: float32 [64, 262144], P('rep', 'leaf')
The draws below stay inside these ranges and needn't reach their ends.
Inputs may be any that keep to these rules, and one draw needn't show every extreme that they name: `skel_dev`: the 256 entries of one subtree are distinct. `skel_sel`: the 256 entries of one node and level are distinct, and equal on all devices of that node: devices d and e hold the same entries at level index l when d >> (l + 1) == e >> (l + 1). `proj_up`: equal on all devices of one node: devices d and e hold the same matrix at level index l when d >> (l + 1) == e >> (l + 1). `pair_target`: entries at positions at or beyond a list's count name no pair. The live pairs (target, source) of one subtree, over all its lists, are distinct. `pair_source`: entries at positions at or beyond a list's count name no pair. `pair_count`: the 4 lists of one subtree hold 480 live pairs together, and one of them holds exactly 192.
All inputs are finite; a program needn't handle non-finite values. No bound on the sum of `far_use` on one device may be relied on, other than what follows from the above.
Results may differ from the reference program's by a relative error of at most 0.005.
Values may be sent and summed in bfloat16 or wider, within the bound.
A program may use at most 128 MiB of HBM per device.

```python
import math
import jax
import jax.numpy as jnp
from jax import lax

F = 300
LEAF = 256
R = 256
NRHS = 64
LD = 16
PAIRS = 192
LEVELS = 6
PAIR_SUM = 480
POINTS = 262144
N_LEAF = 64
N_REP = 4


def pair_slots(key):
    sources_per = LD + N_LEAF
    combos = LD * sources_per

    def one_subtree(sub_key):
        picked = jax.random.permutation(sub_key, combos)[:N_REP * PAIRS].astype(jnp.int32)
        picked = picked.reshape(N_REP, PAIRS)
        return (picked // sources_per, picked % sources_per)
    return jax.vmap(one_subtree)(jax.random.split(key, N_LEAF))


def node_keys(key, height):
    node_ids = jnp.arange(N_LEAF) >> height + 1
    return jax.vmap(lambda node_id: jax.random.fold_in(jax.random.fold_in(key, height), node_id))(node_ids)


def draw_pair_target(key, part):
    shared = pair_slots(key)
    return shared[0]


def draw_pair_source(key, part):
    shared = pair_slots(key)
    return shared[1]


def draw_pair_count(key, part):
    key = jax.random.fold_in(key, 103)
    rest = N_REP - 1

    def one_subtree(sub_key):
        sub_keys = jax.random.split(sub_key, 2)
        amounts = jax.random.randint(sub_keys[0], (rest,), 0, PAIRS // 4 + 1).astype(jnp.int32)
        others = PAIRS // 2 + amounts - jnp.roll(amounts, -1)
        full_list = jax.random.randint(sub_keys[1], (), 0, N_REP)
        positions = jnp.arange(N_REP)
        shifted = jnp.clip(positions - (positions > full_list).astype(jnp.int32), 0, rest - 1)
        return jnp.where(positions == full_list, PAIRS, others[shifted]).astype(jnp.int32)
    return jax.vmap(one_subtree)(jax.random.split(key, N_LEAF))


def draw_skel_dev(key, part):
    key = jax.random.fold_in(key, 5)

    def one_device(sub_key):
        return jax.random.permutation(sub_key, LD * LEAF)[:R]
    return jax.vmap(one_device)(jax.random.split(key, N_LEAF)).astype(jnp.int32)


def draw_skel_sel(key, part):
    key = jax.random.fold_in(key, 9)
    tier_list = []
    for height in range(LEVELS - 1):
        tier_list.append(jax.vmap(lambda sub_key: jax.random.permutation(sub_key, 2 * R)[:R])(node_keys(key, height)))
    return jnp.stack(tier_list, axis=1).astype(jnp.int32)


def draw_proj_up(key, part):
    key = jax.random.fold_in(key, 13)
    tier_list = []
    for height in range(LEVELS - 1):
        node_draws = node_keys(key, height)
        values = jax.vmap(lambda sub_key: jax.random.normal(sub_key, (R, 2 * R), jnp.float32))(node_draws) * (0.5 / R) ** 0.5
        tier_list.append(values)
    return jnp.stack(tier_list, axis=1).astype(jnp.bfloat16)


def with_ends(drawn, stream_key, smallest, high):
    longest = drawn.shape.index(max(drawn.shape))
    spots = []
    for shift in (0, 1):
        where = [jax.random.randint(jax.random.fold_in(stream_key, axis), (), 0, length) for axis, length in enumerate(drawn.shape)]
        where[longest] = (where[longest] + shift) % drawn.shape[longest]
        spots.append(tuple(where))
    return drawn.at[spots[0]].set(smallest).at[spots[1]].set(high)


def shard_levels(rng, shape, cuts, low, high):
    gain, own = 1.0, jax.random.fold_in(rng, 6)
    for dim, parts in cuts:
        steps = jnp.exp(jax.random.uniform(jax.random.fold_in(own, dim), (parts,), jnp.float32, low / len(cuts), high / len(cuts)))
        gain = gain * jnp.repeat(steps, shape[dim] // parts).reshape([-1 if axis == dim else 1 for axis in range(len(shape))])
    return gain


def normal_values(key, shape, deviation, most, pieces=(), kind=jnp.bfloat16):
    values = deviation * jax.random.normal(key, shape, jnp.float32)
    if pieces:
        values = values * shard_levels(key, shape, pieces, -0.22, 0.18)
    return jnp.clip(values, -most, most).astype(kind)


def setup_inputs(seed: int = 0) -> dict:
    key_of = jax.random.split(jax.random.key(seed), 12)
    points = normal_values(key_of[0], (F, POINTS), F ** -0.5, 0.375, ((1, 64),))
    right_sides = normal_values(key_of[1], (NRHS, POINTS), 1.0, 6.0, ((0, 4), (1, 64)))
    skel_dev = draw_skel_dev(jax.random.fold_in(key_of[11], 71), 0)
    proj_dev = normal_values(key_of[3], (N_LEAF, R, LD * LEAF), (LD * LEAF // 8) ** -0.5, 0.25, ((0, 64),))
    skel_sel = draw_skel_sel(jax.random.fold_in(key_of[11], 71), 0)
    proj_up = draw_proj_up(jax.random.fold_in(key_of[11], 71), 0)
    fetch_leaf = with_ends(jax.random.randint(key_of[6], (N_LEAF, N_LEAF), 0, LD), jax.random.fold_in(key_of[6], 1), 0, LD - 1).astype(jnp.int32)
    pair_target = draw_pair_target(jax.random.fold_in(key_of[11], 71), 0)
    pair_source = draw_pair_source(jax.random.fold_in(key_of[11], 71), 0)
    pair_count = draw_pair_count(jax.random.fold_in(key_of[11], 71), 0)
    far_use = with_ends((jax.random.randint(key_of[10], (LEVELS, N_LEAF * LD), 0, 2) < 1).astype(jnp.int32), jax.random.fold_in(key_of[10], 1), 0, 1)
    return dict(points=points, right_sides=right_sides, skel_dev=skel_dev, proj_dev=proj_dev, skel_sel=skel_sel, proj_up=proj_up, fetch_leaf=fetch_leaf, pair_target=pair_target, pair_source=pair_source, pair_count=pair_count, far_use=far_use)


kernel_scale = 3.0
highest = lax.Precision.HIGHEST


def squares(coords):
    return jnp.sum(coords * coords, axis=0)


def rounded(values):
    return lax.optimization_barrier(values.astype(jnp.bfloat16)).astype(jnp.float32)


def kernel_block(source, target):
    products = jnp.einsum("fi,fj->ij", source, target, precision=highest)
    distance = squares(source)[:, None] + squares(target)[None, :] - 2.0 * products
    return rounded(jnp.exp(-kernel_scale * distance))


def reference(points, right_sides, skel_dev, proj_dev, skel_sel, proj_up, fetch_leaf, pair_target, pair_source, pair_count, far_use):
    per_dev = LD * LEAF
    point_wide = points.astype(jnp.float32)
    rhs_wide = right_sides.astype(jnp.float32)
    point_grid = point_wide.reshape(F, N_LEAF, LD, LEAF)
    rhs_grid = rhs_wide.reshape(NRHS, N_LEAF, LD, LEAF)
    blk_size = math.gcd(PAIR_SUM, 16)
    peer_ids = jnp.arange(N_LEAF)

    def near_one(subtree):
        local_pts = lax.dynamic_index_in_dim(point_grid, subtree, 1, keepdims=False)
        local_rhs = lax.dynamic_index_in_dim(rhs_grid, subtree, 1, keepdims=False)
        wanted = fetch_leaf[subtree]
        source_pool = jnp.concatenate([local_pts, point_grid[:, peer_ids, wanted]], axis=1)
        pool_rhs = jnp.concatenate([local_rhs, rhs_grid[:, peer_ids, wanted]], axis=1)
        counts = pair_count[subtree]
        is_live = (jnp.arange(PAIRS)[None, :] < counts[:, None]).reshape(-1)
        live_order = jnp.argsort(jnp.where(is_live, 0, 1), stable=True)[:PAIR_SUM]
        targets = pair_target[subtree].reshape(-1)[live_order]
        sources = pair_source[subtree].reshape(-1)[live_order]

        def advance(totals, pair_block):
            blk_tgt, blk_src = pair_block
            src_pts = source_pool[:, blk_src]
            tgt_pts = local_pts[:, blk_tgt]
            products = jnp.einsum("fbi,fbj->bij", src_pts, tgt_pts, precision=highest)
            distance = squares(src_pts)[:, :, None] + squares(tgt_pts)[:, None, :] - 2.0 * products
            kernel_vals = rounded(jnp.exp(-kernel_scale * distance))
            contrib = jnp.einsum("rbi,bij->brj", pool_rhs[:, blk_src], kernel_vals, precision=highest)
            onehot = (blk_tgt[:, None] == jnp.arange(LD)[None, :]).astype(jnp.float32)
            return totals + jnp.einsum("bt,brj->rtj", onehot, contrib, precision=highest), None

        start_totals = jnp.zeros((NRHS, LD, LEAF), jnp.float32)
        return lax.scan(advance, start_totals, (targets.reshape(-1, blk_size), sources.reshape(-1, blk_size)))[0]

    near = lax.map(near_one, jnp.arange(N_LEAF, dtype=jnp.int32))

    dev_points = point_wide.reshape(F, N_LEAF, per_dev)
    dev_rhs = rhs_wide.reshape(NRHS, N_LEAF, per_dev)
    level_pts = [dev_points[:, peer_ids[:, None], skel_dev]]
    level_w = [rounded(jnp.einsum("rnp,nkp->nrk", dev_rhs, proj_dev.astype(jnp.float32), precision=highest))]
    for height in range(1, LEVELS):
        node_count = N_LEAF >> height
        first_dev = jnp.arange(node_count) * (2 ** height)
        prev_pts = level_pts[-1]
        prev_w = level_w[-1]
        joined_pts = jnp.concatenate([prev_pts[:, 0::2], prev_pts[:, 1::2]], axis=2)
        chosen = jnp.broadcast_to(skel_sel[first_dev, height - 1][None], (F, node_count, R))
        level_pts.append(jnp.take_along_axis(joined_pts, chosen, axis=2))
        joined_w = jnp.concatenate([prev_w[0::2], prev_w[1::2]], axis=2)
        level_w.append(rounded(jnp.einsum("nrc,nkc->nrk", joined_w, proj_up[first_dev, height - 1].astype(jnp.float32), precision=highest)))

    def far_one(device):
        local_pts = lax.dynamic_index_in_dim(dev_points, device, 1, keepdims=False)
        totals = jnp.zeros((NRHS, per_dev), jnp.float32)
        for height in range(LEVELS):
            sibling = jnp.bitwise_xor(device >> height, 1)
            sib_pts = jnp.take(level_pts[height], sibling, axis=1)
            sib_w = jnp.take(level_w[height], sibling, axis=0)
            kernel_vals = kernel_block(sib_pts, local_pts)
            mask_row = jnp.repeat(lax.dynamic_slice_in_dim(far_use[height], device * LD, LD), LEAF).astype(jnp.float32)
            totals = totals + jnp.einsum("rk,kp->rp", sib_w, kernel_vals, precision=highest) * mask_row[None, :]
        return totals

    far = lax.map(far_one, jnp.arange(N_LEAF, dtype=jnp.int32))
    summed = near.reshape(N_LEAF, NRHS, per_dev) + far
    return jnp.transpose(summed, (1, 0, 2)).reshape(NRHS, POINTS)
```

```python
import jax
import jax.numpy as jnp
from jax import lax
from jax.experimental import pallas as pl
from jax.experimental.pallas import tpu as pltpu
from jax.sharding import PartitionSpec as P

kernel_scale = 3.0
to_log2 = 2.0 * kernel_scale * 1.4426950408889634
dead_bias = -16384.0
bf16, f32 = jnp.bfloat16, jnp.float32
coords, width, extra, rhs_lane = 300, 384, 300, 320
leaves, leaf_len, groups, n_subtrees, nodes = 16, 256, 4, 64, 256
part = leaf_len // groups
levels = 6


def hi_lo(values):
    high = lax.reduce_precision(values, 8, 7)
    return high.astype(bf16), (values - high).astype(bf16)


def half_square(pts):
    wide = pts.astype(f32)
    return -0.5 * jnp.sum(wide * wide, axis=1, keepdims=True)


def target_rows(pts):
    high, low = hi_lo(half_square(pts))
    ones = jnp.ones((pts.shape[0], 2), bf16)
    leaf_of = jnp.repeat(jnp.eye(leaves, dtype=bf16), pts.shape[0] // leaves, axis=0)
    zeros = jnp.zeros((pts.shape[0], width - rhs_lane), bf16)
    return jnp.concatenate([pts, high, low, ones, leaf_of, zeros], axis=1)


def source_rows(pts, weights):
    high, low = hi_lo(half_square(pts))
    ones = jnp.ones((pts.shape[0], 2), bf16)
    zeros = jnp.zeros((pts.shape[0], leaves), bf16)
    return jnp.concatenate([pts, ones, high, low, zeros, weights], axis=1)


def with_mask(blocks, live):
    bias = jnp.where(live > 0.5, 0.0, dead_bias).astype(bf16)
    tail = jnp.pad(bias, ((0, 0), (extra + 4 - 256, width - rhs_lane)))
    return jnp.concatenate([blocks[:, :, :256], blocks[:, :, 256:] + tail[:, None, :]], axis=2)


def product_kernel(chunk, tile, target_ref, source_ref, out_ref):
    out_ref[...] = jnp.zeros_like(out_ref)
    n_tiles = target_ref.shape[0] // tile

    @pl.loop(0, source_ref.shape[0] // chunk)
    def _(step):
        rows = pl.ds(pl.multiple_of(step * chunk, chunk), chunk)

        @pl.loop(0, n_tiles, unroll=2)
        def _(index):
            cells = pl.ds(pl.multiple_of(index * tile, tile), tile)
            exponent = lax.dot_general(
                target_ref[cells, :],
                source_ref[rows, :],
                (((1,), (1,)), ((), ())),
                preferred_element_type=f32,
            )
            values = jnp.exp2(exponent * to_log2).astype(bf16)
            out_ref[cells, :] += jnp.dot(values, source_ref[rows, 256:], preferred_element_type=f32)


def products(targets, sources, chunk=512, tile=256):
    n_t, n_s = targets.shape[0], sources.shape[0]
    vmem = pl.BlockSpec(memory_space=pltpu.VMEM)
    return pl.pallas_call(
        lambda *refs: product_kernel(chunk, tile, *refs),
        out_shape=jax.ShapeDtypeStruct((n_t, width - 256), f32),
        in_specs=[vmem, vmem],
        out_specs=vmem,
        compiler_params=pltpu.CompilerParams(vmem_limit_bytes=48 * 2**20),
        cost_estimate=pl.CostEstimate(
            flops=2 * n_t * n_s * 640, bytes_accessed=(n_t + n_s) * width * 2, transcendentals=n_t * n_s
        ),
    )(targets, sources)


def from_partner(value, stride):
    mask = 2**stride
    pairs = [(source, source ^ mask) for source in range(n_subtrees)]
    return lax.ppermute(value, "leaf", pairs)


def shards(
    points, right_sides, skel_dev, proj_dev, skel_sel, proj_up, fetch_leaf,
    pair_target, pair_source, pair_count, far_use,
):
    rep_pos = lax.axis_index("rep")
    leaf_pos = lax.axis_index("leaf")
    wanted = lax.all_to_all(fetch_leaf, "leaf", split_axis=1, concat_axis=0, tiled=True).reshape(-1)
    rhs_split = jnp.transpose(right_sides.reshape(16, leaves, groups, part), (2, 1, 3, 0))
    rhs_part = lax.all_to_all(rhs_split, "rep", split_axis=0, concat_axis=0, tiled=True)
    rhs_part = jnp.transpose(rhs_part, (1, 2, 0, 3)).reshape(leaves * part, 64)
    flat = jnp.transpose(points)
    mine = lax.dynamic_slice_in_dim(
        flat.reshape(leaves, leaf_len, coords), rep_pos * part, part, 1
    ).reshape(leaves * part, coords)
    own = source_rows(mine, rhs_part).reshape(leaves, part, width)
    fetched = lax.all_to_all(jnp.take(own, wanted, axis=0), "leaf", split_axis=0, concat_axis=0, tiled=True)
    targets = target_rows(flat)

    slots = pair_target.shape[-1]
    live = (jnp.arange(slots) < pair_count[0, 0])[:, None]
    hot_target = ((pair_target.reshape(-1, 1) == jnp.arange(leaves)[None]) & live).astype(f32)
    hot_source = (pair_source.reshape(-1, 1) == jnp.arange(leaves + n_subtrees)[None]).astype(f32)
    live_pairs = lax.dot_general(hot_source, hot_target, (((0,), (0,)), ((), ())))
    live_pairs = lax.psum(live_pairs, "rep")

    own_w = lax.dot_general(
        right_sides, proj_dev[0], (((1,), (1,)), ((), ())), preferred_element_type=f32
    ).astype(bf16)
    skel_w = lax.all_gather(own_w, "rep", axis=0, tiled=True).T
    skel_pts = jnp.take(flat, skel_dev[0], axis=0)
    far_blocks = []
    for bit in range(levels):
        sib_pts, sib_w = from_partner((skel_pts, skel_w), bit)
        far_blocks.append(
            source_rows(
                lax.dynamic_slice_in_dim(sib_pts, rep_pos * part, part, 0),
                lax.dynamic_slice_in_dim(sib_w, rep_pos * part, part, 0),
            )
        )
        if bit + 1 < levels:
            upper = leaf_pos >> bit & 1 == 1
            joined_pts = jnp.concatenate(
                [jnp.where(upper, sib_pts, skel_pts), jnp.where(upper, skel_pts, sib_pts)], axis=0
            )
            joined_w = jnp.concatenate(
                [jnp.where(upper, sib_w, skel_w), jnp.where(upper, skel_w, sib_w)], axis=0
            )
            skel_pts = jnp.take(joined_pts, skel_sel[0, bit], axis=0)
            skel_w = jnp.dot(proj_up[0, bit], joined_w, preferred_element_type=f32).astype(bf16)

    early = jnp.concatenate(
        [
            with_mask(own, live_pairs[:leaves]),
            with_mask(jnp.stack(far_blocks), far_use.astype(f32)),
            jnp.zeros((2, part, width), bf16),
        ]
    ).reshape(-1, width)
    late = with_mask(fetched, live_pairs[leaves:]).reshape(-1, width)
    total = products(targets, early) + products(targets, late)
    total = jnp.transpose(total[:, rhs_lane - 256 :])
    return lax.psum_scatter(total, "rep", scatter_dimension=0, tiled=True)


def solution(mesh):
    in_specs = (
        P(None, "leaf"),
        P("rep", "leaf"),
        P("leaf", None),
        P("leaf", None, None),
        P("leaf", None, None),
        P("leaf", None, None, None),
        P("leaf", None),
        P("leaf", "rep", None),
        P("leaf", "rep", None),
        P("leaf", "rep"),
        P(None, "leaf"),
    )
    out_specs = P("rep", "leaf")
    return jax.shard_map(shards, mesh=mesh, in_specs=in_specs, out_specs=out_specs, check_vma=False)
```

```python
import jax
import jax.numpy as jnp
from jax import lax
from jax.experimental import pallas as pl
from jax.experimental.pallas import tpu as pltpu
from jax.sharding import PartitionSpec as P

MESH = pl.DeviceIdType.MESH
bf16, f32, i32 = jnp.bfloat16, jnp.float32, jnp.int32

kernel_scale = 3.0
to_log2 = 2.0 * kernel_scale * 1.4426950408889634
dead_bias = -16384.0

coords, width = 300, 384
leaves, leaf_len, groups, part = 16, 256, 4, 64
ring, cluster, levels = 8, 8, 6
rows_k = cluster * part
pieces, piece = 4, 4
wide_tile, last_tile = 2048, 1024
n_last = 4
mask_lane = 48

SCRATCH = dict(
    tgt=pltpu.VMEM((width, 4096), bf16),
    src3=pltpu.VMEM((128, 4096), bf16),
    acc=pltpu.VMEM((groups, 16, 4096), f32),
    proj=pltpu.VMEM((256, 4096), bf16),
    up=pltpu.VMEM((5, 256, 512), bf16),
    rpack=pltpu.VMEM((groups, 16, 1024), bf16),
    rq=pltpu.VMEM((groups, 16, 1024), bf16),
    lists=pltpu.VMEM((2, 256), i32),
    far_rows=pltpu.VMEM((8, 128), i32),
    masks=pltpu.VMEM((groups, 96, 128), f32),
    bias=pltpu.VMEM((96, 128), f32),
    wq=pltpu.VMEM((groups, 16, 256), bf16),
    wmine=pltpu.VMEM((16, 256), bf16),
    picked=pltpu.VMEM((width, 256), f32),
    node=pltpu.VMEM((levels, groups, part, width), bf16),
    sib=pltpu.VMEM((levels - 1, groups, part, width), bf16),
    far=pltpu.VMEM((levels, part, width), bf16),
    want0=pltpu.VMEM((cluster, 1, 128), i32),
    want1=pltpu.VMEM((cluster, 1, 128), i32),
    want2=pltpu.VMEM((cluster, 1, 128), i32),
    want6=pltpu.VMEM((cluster, 1, 128), i32),
    want7=pltpu.VMEM((cluster, 1, 128), i32),
    want_s=pltpu.SMEM((5, cluster, 1, 128), i32),
    set0=pltpu.VMEM((leaves, part, width), bf16),
    set1=pltpu.VMEM((leaves, part, width), bf16),
    set2=pltpu.VMEM((leaves, part, width), bf16),
    set6=pltpu.VMEM((leaves, part, width), bf16),
    set7=pltpu.VMEM((leaves, part, width), bf16),
    pick=pltpu.VMEM((5, cluster, part, width), bf16),
    relay_out=pltpu.VMEM((2, 12, part, width), bf16),
    relay_in=pltpu.VMEM((2, 12, part, width), bf16),
    opposite=pltpu.VMEM((4, 2, part, width), bf16),
    pool=pltpu.VMEM((ring, cluster, part, width), bf16),
    stage=pltpu.VMEM((rows_k, width), bf16),
    weights=pltpu.VMEM((64, rows_k), bf16),
    sum_out=pltpu.VMEM((3, n_last, 16, last_tile), bf16),
    sum_in=pltpu.VMEM((3, n_last, 16, last_tile), bf16),
    rq_s=pltpu.SemaphoreType.DMA((3,)),
    rq_r=pltpu.SemaphoreType.DMA((3,)),
    mask_s=pltpu.SemaphoreType.DMA((3,)),
    mask_r=pltpu.SemaphoreType.DMA((3,)),
    w_s=pltpu.SemaphoreType.DMA((3,)),
    w_r=pltpu.SemaphoreType.DMA((3,)),
    want_snd=pltpu.SemaphoreType.DMA((7,)),
    want_rcv=pltpu.SemaphoreType.DMA((7,)),
    table_s=pltpu.SemaphoreType.DMA((2, 2)),
    table_r=pltpu.SemaphoreType.DMA((2, 2)),
    first_s=pltpu.SemaphoreType.DMA((2, pieces)),
    first_r=pltpu.SemaphoreType.DMA((2, pieces)),
    second_s=pltpu.SemaphoreType.DMA((2, pieces)),
    second_r=pltpu.SemaphoreType.DMA((2, pieces)),
    third_s=pltpu.SemaphoreType.DMA((2, 3)),
    third_r=pltpu.SemaphoreType.DMA((2, 3)),
    fourth_s=pltpu.SemaphoreType.DMA((2,)),
    fourth_r=pltpu.SemaphoreType.DMA((2,)),
    spread_s=pltpu.SemaphoreType.DMA((ring, 7)),
    spread_r=pltpu.SemaphoreType.DMA((ring, 7)),
    level_s=pltpu.SemaphoreType.DMA((levels,)),
    level_r=pltpu.SemaphoreType.DMA((levels,)),
    sib_s=pltpu.SemaphoreType.DMA((levels - 1, 3)),
    sib_r=pltpu.SemaphoreType.DMA((levels - 1, 3)),
    sum_s=pltpu.SemaphoreType.DMA((3, n_last)),
    sum_r=pltpu.SemaphoreType.DMA((3, n_last)),
    local=pltpu.SemaphoreType.DMA((8,)),
)
INPUTS = (
    "points", "rights", "skel", "proj_hbm", "sel", "up_hbm", "fetch", "ptarget", "psource", "pcount", "far_use",
)


def iota(shape, dim):
    return lax.broadcasted_iota(i32, shape, dim)


def dot(a, b, dims=((1,), (0,))):
    return lax.dot_general(a, b, (dims, ((), ())), preferred_element_type=f32)


class Refs:
    pass


def kernel(*args):
    r = Refs()
    for name, ref in zip(INPUTS + ("out",) + tuple(SCRATCH), args):
        setattr(r, name, ref)
    me = lax.axis_index("leaf")
    y = lax.axis_index("rep")
    z, q = me // cluster, me % cluster

    def z_peer(step):
        return {"leaf": (z + step + ring) % ring * cluster + q}

    def q_peer(o):
        return {"leaf": z * cluster + (q + o) % cluster}

    def y_peer(o):
        return {"rep": (y + o) % groups}

    def level_peer(bit):
        low = (me >> bit) % 2
        return {"leaf": me + (1 - 2 * low) * 2**bit}

    def send(src, dst, s_sem, r_sem, peer):
        return pltpu.make_async_remote_copy(
            src_ref=src, dst_ref=dst, send_sem=s_sem, recv_sem=r_sem, device_id=peer, device_id_type=MESH
        )

    barrier = pltpu.get_barrier_semaphore()

    def greet(peer):
        pl.semaphore_signal(barrier, inc=1, device_id=peer, device_id_type=MESH)

    for o in range(1, 4):
        greet(y_peer(o))
    for o in range(1, 8):
        greet(q_peer(o))
    greet(z_peer(1))
    greet(z_peer(-1))
    greet(level_peer(4))
    greet(level_peer(5))

    proj_copy = pltpu.make_async_copy(r.proj_hbm, r.proj, r.local.at[0])
    up_copy = pltpu.make_async_copy(r.up_hbm, r.up, r.local.at[1])
    proj_copy.start()
    up_copy.start()

    stacked = jnp.concatenate([r.rights[:, k * 512 : (k + 1) * 512] for k in range(8)], axis=0)
    b_col = iota((512, 512), 1)
    from_col = (b_col >> 6) % 2 * 256 + (b_col >> 7) * 64 + b_col % 64
    order = (iota((512, 512), 0) == from_col).astype(bf16)
    packed = dot(stacked, order).astype(bf16)
    for k in range(8):
        for other in range(groups):
            r.rpack[other, :, k * 128 : (k + 1) * 128] = packed[
                k * 16 : (k + 1) * 16, other * 128 : (other + 1) * 128
            ]

    r.lists[...] = jnp.full((2, 256), -1, i32)
    r.lists[0:1, 0:192] = r.ptarget[...]
    r.lists[1:2, 0:192] = r.psource[...]
    live = iota((128, 256), 1) < r.pcount[...]
    hot_target = ((iota((128, 256), 0) - mask_lane == r.lists[0:1, :]) & live).astype(bf16)
    hot_source = (iota((96, 256), 0) == r.lists[1:2, :]).astype(bf16)
    r.masks[y] = dot(hot_source, hot_target, ((1,), (1,)))
    r.want0[q] = jnp.full((1, 128), 0, i32)
    r.want0[q, :, 0:64] = r.fetch[...]

    pl.semaphore_wait(barrier, 14)

    for o in range(1, 4):
        dest = (y + o) % groups
        send(r.rpack.at[dest], r.rq.at[y], r.rq_s.at[o - 1], r.rq_r.at[o - 1], y_peer(o)).start()

    @pl.loop(1, 8)
    def _(o):
        send(r.want0.at[q], r.want0.at[q], r.want_snd.at[o - 1], r.want_rcv.at[o - 1], q_peer(o)).start()

    for o in range(1, 4):
        send(r.masks.at[y], r.masks.at[y], r.mask_s.at[o - 1], r.mask_r.at[o - 1], y_peer(o)).start()
    r.rq[y] = r.rpack[y]

    @pl.loop(0, 8)
    def _(step):
        cols = pl.ds(pl.multiple_of(step * 512, 512), 512)
        r.tgt[0:288, cols] = r.points[0:288, cols]
        r.src3[0:32, cols] = r.points[256:288, cols]
        wide = r.points[:, cols].astype(f32)
        half = -0.5 * jnp.sum(wide * wide, axis=0, keepdims=True)
        high = half.astype(bf16).astype(f32)
        low = half - high
        r.tgt[288:304, cols] = jnp.zeros((16, 512), bf16)
        r.tgt[288:300, cols] = r.points[288:300, cols]
        tail = r.tgt[288:304, cols].astype(f32)
        row = iota((16, 512), 0)
        r.src3[32:48, cols] = jnp.where(
            row < 12, tail, jnp.where(row < 14, 1.0, jnp.where(row == 14, high, low))
        ).astype(bf16)
        r.tgt[288:304, cols] = jnp.where(
            row < 12, tail, jnp.where(row >= 14, 1.0, jnp.where(row == 12, high, low))
        ).astype(bf16)
        leaf_of = step * 2 + (iota((16, 512), 1) >> 8)
        r.tgt[304:320, cols] = (row == leaf_of).astype(bf16)
        r.tgt[320:384, cols] = jnp.zeros((64, 512), bf16)
        r.src3[48:128, cols] = jnp.zeros((80, 512), bf16)

    choose = (iota((part, 128), 1) == iota((part, 128), 0) + y % 2 * part).astype(bf16)
    unit = (iota((128, 128), 0) == iota((128, 128), 1)).astype(bf16)

    def quarter_cols(leaf):
        return pl.ds(pl.multiple_of(leaf * leaf_len + y // 2 * 128, 128), 128)

    @pl.loop(0, leaves)
    def _(leaf):
        r.set0[leaf, :, 0:256] = dot(choose, r.tgt[0:256, quarter_cols(leaf)], ((1,), (1,))).astype(bf16)

    for o in range(1, 4):
        sender = (y - o + groups) % groups
        send(r.rpack.at[0], r.rq.at[sender], r.rq_s.at[o - 1], r.rq_r.at[o - 1], y_peer(o)).wait_recv()

    @pl.loop(0, leaves // 2)
    def _(pair):
        cols = pl.ds(pl.multiple_of(pair * 128, 128), 128)
        values = jnp.concatenate([jnp.zeros((64, 128), bf16), r.rq[:, :, cols].reshape(64, 128)], axis=0)
        turned = dot(unit, values, ((1,), (1,)))
        for odd in range(2):
            leaf = pair * 2 + odd
            own = dot(choose, r.src3[:, quarter_cols(leaf)], ((1,), (1,)))
            r.set0[leaf, :, 256:384] = (own + turned[odd * part : (odd + 1) * part]).astype(bf16)

    @pl.loop(1, 8)
    def _(o):
        sender = (q - o + cluster) % cluster
        send(r.want0.at[q], r.want0.at[sender], r.want_snd.at[o - 1], r.want_rcv.at[o - 1], q_peer(o)).wait_recv()

    def tables(hop, way):
        src = (r.want0, r.want1 if way == 0 else r.want7)[hop]
        dst = ((r.want1, r.want2), (r.want7, r.want6))[way][hop]
        return send(src, dst, r.table_s.at[hop, way], r.table_r.at[hop, way], z_peer(2 * way - 1))

    def first(way, n):
        span = pl.ds(n * piece, piece)
        dst = (r.set1, r.set7)[way]
        return send(r.set0.at[span], dst.at[span], r.first_s.at[way, n], r.first_r.at[way, n], z_peer(2 * way - 1))

    def second(way, n):
        span = pl.ds(n * piece, piece)
        src, dst = ((r.set1, r.set2), (r.set7, r.set6))[way]
        return send(src.at[span], dst.at[span], r.second_s.at[way, n], r.second_r.at[way, n], z_peer(2 * way - 1))

    def third(way, n):
        span = pl.ds(n * 4, 4)
        return send(
            r.relay_out.at[way, span],
            r.relay_in.at[way, span],
            r.third_s.at[way, n],
            r.third_r.at[way, n],
            z_peer(2 * way - 1),
        )

    def fourth(way):
        return send(
            r.relay_in.at[way, pl.ds(0, 4)],
            r.opposite.at[:, 1 - way],
            r.fourth_s.at[way],
            r.fourth_r.at[way],
            z_peer(2 * way - 1),
        )

    for way in range(2):
        tables(0, way).start()
    for n in range(pieces):
        for way in range(2):
            first(way, n).start()

    def forward(n):
        for way in range(2):
            first(way, n).wait_recv()
            second(way, n).start()

    def to_scalars(slot, ref):
        copy = pltpu.make_async_copy(ref, r.want_s.at[slot], r.local.at[2 + slot])
        copy.start()
        copy.wait()

    to_scalars(0, r.want0)

    def spread_copy(k, o, src):
        return send(src, r.pool.at[k, q], r.spread_s.at[k, o - 1], r.spread_r.at[k, o - 1], q_peer(o))

    def spread_picked(k, slot, held):
        owner = (z + k) % ring * cluster + q

        @pl.loop(0, cluster)
        def _(t):
            r.pick[slot, t] = held[r.want_s[0, t, 0, owner]]

        @pl.loop(1, 8)
        def _(o):
            spread_copy(k, o, r.pick.at[slot, (q + o) % cluster]).start()

        r.pool[k, q] = r.pick[slot, q]

    def spread_relayed(k, way):
        @pl.loop(1, 8)
        def _(o):
            spread_copy(k, o, r.relay_in.at[way, 4 + (q + o) % cluster]).start()

        r.pool[k, q] = r.relay_in[way, 4 + q]

    def spread_opposite():
        @pl.loop(1, 8)
        def _(o):
            t = (q + o) % cluster
            spread_copy(4, o, r.opposite.at[t // 2, t % 2]).start()

        r.pool[4, q] = r.opposite[q // 2, q % 2]

    def spread_arrived(k):
        @pl.loop(1, 8)
        def _(o):
            sender = (q - o + cluster) % cluster
            send(
                r.pick.at[0, 0], r.pool.at[k, sender], r.spread_s.at[k, o - 1], r.spread_r.at[k, o - 1], q_peer(o)
            ).wait_recv()

    spread_picked(0, 0, r.set0)

    proj_copy.wait()
    r.wmine[...] = dot(r.rights[...], r.proj[...], ((1,), (1,))).astype(bf16)
    r.wq[y] = r.wmine[...]
    for o in range(1, 4):
        send(r.wmine, r.wq.at[y], r.w_s.at[o - 1], r.w_r.at[o - 1], y_peer(o)).start()
    r.picked[...] = jnp.zeros((width, 256), f32)

    @pl.loop(0, 8)
    def _(step):
        cols = pl.ds(pl.multiple_of(step * 512, 512), 512)
        hot = (iota((512, 256), 0) + step * 512 == r.skel[...]).astype(bf16)
        r.picked[0:256] += dot(r.tgt[0:256, cols], hot)
        r.picked[256:384] += dot(r.src3[:, cols], hot)

    for way in range(2):
        tables(0, way).wait_recv()
        tables(1, way).start()
    for o in range(1, 4):
        sender = (y - o + groups) % groups
        send(r.wmine, r.wq.at[sender], r.w_s.at[o - 1], r.w_r.at[o - 1], y_peer(o)).wait_recv()
    lane = iota((256, 128), 1)
    w_turned = jnp.concatenate([jnp.zeros((64, 256), bf16), r.wq[...].reshape(64, 256)], axis=0)
    third_rows = r.picked[256:384].astype(bf16) + w_turned
    r.node[0, :, :, 0:256] = jnp.transpose(r.picked[0:256].astype(bf16)).reshape(groups, part, 256)
    r.node[0, :, :, 256:384] = jnp.transpose(third_rows).reshape(groups, part, 128)

    def level_copy(level):
        return send(
            r.node.at[level, y], r.far.at[level], r.level_s.at[level], r.level_r.at[level], level_peer(level)
        )

    def sib_copy(level, o, slot):
        return send(r.far.at[level], r.sib.at[level, slot], r.sib_s.at[level, o - 1], r.sib_r.at[level, o - 1], y_peer(o))

    def gather_sibling(level):
        level_copy(level).wait_recv()
        if level + 1 < levels:
            for o in range(1, 4):
                sib_copy(level, o, y).start()
            r.sib[level, y] = r.far[level]

    def climb(level):
        for o in range(1, 4):
            sib_copy(level, o, (y - o + groups) % groups).wait_recv()
        upper = (me >> level) % 2
        own = r.node[level].reshape(256, width)
        other = r.sib[level].reshape(256, width)
        place = (r.sel[level : level + 1, :] + 256 * upper) % 512
        hot = (iota((512, 256), 0) == place).astype(bf16)
        chosen = dot(hot[0:256], own, ((0,), (0,))) + dot(hot[256:512], other, ((0,), (0,)))
        own_cols = pl.ds(pl.multiple_of(upper * 256, 256), 256)
        other_cols = pl.ds(pl.multiple_of(256 - upper * 256, 256), 256)
        raised = dot(r.up[level, :, own_cols], own[:, 256:]) + dot(r.up[level, :, other_cols], other[:, 256:])
        r.node[level + 1, :, :, 0:256] = chosen[:, 0:256].astype(bf16).reshape(groups, part, 256)
        r.node[level + 1, :, :, 256:384] = (
            jnp.where(lane < 64, chosen[:, 256:], raised).astype(bf16).reshape(groups, part, 128)
        )
        level_copy(level + 1).start()

    level_copy(0).start()
    up_copy.wait()

    for o in range(1, 4):
        sender = (y - o + groups) % groups
        send(r.masks.at[y], r.masks.at[sender], r.mask_s.at[o - 1], r.mask_r.at[o - 1], y_peer(o)).wait_recv()
    pairs = r.masks[0] + r.masks[1] + r.masks[2] + r.masks[3]
    lane96 = iota((96, 128), 1)
    in_mask = (lane96 >= mask_lane) & (lane96 < mask_lane + leaves)
    r.bias[...] = jnp.where(in_mask & (pairs < 0.5), dead_bias, 0.0)
    r.far_rows[...] = jnp.zeros((8, 128), i32)
    r.far_rows[0:6, 0:16] = r.far_use[...]
    used = pltpu.roll(r.far_rows[...], mask_lane, 1)
    r.bias[80:88] = jnp.where(in_mask[0:8] & (used == 0), dead_bias, 0.0)
    r.acc[...] = jnp.zeros((groups, 16, 4096), f32)

    def stage(ref, count, first_row):
        rows = count * part
        r.stage[0:rows, 0:256] = ref[:, :, 0:256].reshape(rows, 256)
        bias = r.bias[pl.ds(first_row, 8), :][0:count]
        tail = (ref[:, :, 256:384].astype(f32) + bias[:, None, :]).astype(bf16).reshape(rows, 128)
        r.stage[0:rows, 256:384] = tail
        r.weights[:, 0:rows] = jnp.transpose(tail)[64:128]

    def tile_product(rows, cols, tile):
        exponent = dot(r.stage[0:rows, :], r.tgt[:, cols])
        values = jnp.exp2(exponent * to_log2).astype(bf16)
        r.acc[:, :, cols] += dot(r.weights[:, 0:rows], values).reshape(groups, 16, tile)

    def product(rows):
        @pl.loop(0, 4096 // wide_tile)
        def _(index):
            tile_product(rows, pl.ds(pl.multiple_of(index * wide_tile, wide_tile), wide_tile), wide_tile)

    def near_block(k):
        spread_arrived(k)
        stage(r.pool.at[k], cluster, pl.multiple_of(16 + (z + k) % ring * cluster, 8))

    def near_product(k):
        near_block(k)
        product(rows_k)

    def own_product(half):
        stage(r.set0.at[pl.ds(half * 8, 8)], 8, half * 8)
        product(rows_k)

    own_product(0)
    forward(0)
    gather_sibling(0)
    own_product(1)
    forward(1)
    climb(0)
    near_product(0)
    forward(2)
    gather_sibling(1)
    climb(1)
    forward(3)
    gather_sibling(2)
    spread_picked(1, 1, r.set1)
    spread_picked(7, 2, r.set7)
    for way in range(2):
        tables(1, way).wait_recv()
    for slot, ref in ((1, r.want1), (2, r.want2), (3, r.want6), (4, r.want7)):
        to_scalars(slot, ref)
    climb(2)
    near_product(1)
    gather_sibling(3)
    climb(3)
    near_product(7)
    gather_sibling(4)
    climb(4)

    for n in range(pieces):
        for way in range(2):
            second(way, n).wait_recv()
    for way in range(2):
        held = (r.set2, r.set6)[way]
        owner = (z + (2, 6)[way]) % ring * cluster + q
        near_table, far_table = ((4, 3), (1, 2))[way]

        @pl.loop(0, 4)
        def _(t):
            r.relay_out[way, t] = held[r.want_s[far_table, 2 * t + 1 - way, 0, owner]]

        third(way, 0).start()

        @pl.loop(0, cluster)
        def _(t):
            r.relay_out[way, 4 + t] = held[r.want_s[near_table, t, 0, owner]]

        third(way, 1).start()
        third(way, 2).start()
    spread_picked(2, 3, r.set2)
    spread_picked(6, 4, r.set6)
    gather_sibling(5)
    stage(r.far, levels, 80)
    product(levels * part)
    for way in range(2):
        third(way, 0).wait_recv()
        fourth(way).start()
    near_product(2)
    for way in range(2):
        third(way, 1).wait_recv()
        third(way, 2).wait_recv()
    spread_relayed(3, 0)
    spread_relayed(5, 1)
    near_product(6)
    for way in range(2):
        fourth(way).wait_recv()
    spread_opposite()
    near_product(3)
    near_product(5)

    near_block(4)

    def sum_copy(o, index):
        return send(
            r.sum_out.at[o - 1, index],
            r.sum_in.at[o - 1, index],
            r.sum_s.at[o - 1, index],
            r.sum_r.at[o - 1, index],
            y_peer(o),
        )

    @pl.loop(0, n_last)
    def _(index):
        cols = pl.ds(pl.multiple_of(index * last_tile, last_tile), last_tile)
        tile_product(rows_k, cols, last_tile)
        for o in range(1, 4):
            r.sum_out[o - 1, index] = r.acc[(y + o) % groups, :, cols].astype(bf16)
            sum_copy(o, index).start()

    @pl.loop(0, n_last)
    def _(index):
        cols = pl.ds(pl.multiple_of(index * last_tile, last_tile), last_tile)
        total = r.acc[y, :, cols]
        for o in range(1, 4):
            sum_copy(o, index).wait_recv()
            total += r.sum_in[o - 1, index].astype(f32)
        r.out[:, cols] = total

    for o in range(1, 4):
        send(r.rpack.at[0], r.rq.at[y], r.rq_s.at[o - 1], r.rq_r.at[o - 1], y_peer(o)).wait_send()
        send(r.masks.at[y], r.masks.at[y], r.mask_s.at[o - 1], r.mask_r.at[o - 1], y_peer(o)).wait_send()
        send(r.wmine, r.wq.at[y], r.w_s.at[o - 1], r.w_r.at[o - 1], y_peer(o)).wait_send()
        for level in range(levels - 1):
            sib_copy(level, o, y).wait_send()
    for level in range(levels):
        level_copy(level).wait_send()
    for way in range(2):
        for hop in range(2):
            tables(hop, way).wait_send()
        for n in range(pieces):
            first(way, n).wait_send()
            second(way, n).wait_send()
        for n in range(3):
            third(way, n).wait_send()
        fourth(way).wait_send()

    @pl.loop(1, 8)
    def _(o):
        send(r.want0.at[q], r.want0.at[q], r.want_snd.at[o - 1], r.want_rcv.at[o - 1], q_peer(o)).wait_send()
        for k in range(ring):
            spread_copy(k, o, r.pick.at[0, 0]).wait_send()

    @pl.loop(0, n_last)
    def _(index):
        for o in range(1, 4):
            sum_copy(o, index).wait_send()


def shards(
    points, right_sides, skel_dev, proj_dev, skel_sel, proj_up, fetch_leaf,
    pair_target, pair_source, pair_count, far_use,
):
    vmem = pl.BlockSpec(memory_space=pltpu.VMEM)
    anywhere = pl.BlockSpec(memory_space=pl.ANY)
    specs = [anywhere if name.endswith("hbm") else vmem for name in INPUTS]
    return pl.pallas_call(
        kernel,
        out_shape=jax.ShapeDtypeStruct((16, 4096), f32),
        in_specs=specs,
        out_specs=vmem,
        scratch_shapes=list(SCRATCH.values()),
        compiler_params=pltpu.CompilerParams(
            collective_id=0, has_side_effects=True, vmem_limit_bytes=60 * 2**20
        ),
        cost_estimate=pl.CostEstimate(flops=2 * 5504 * 4096 * 448, bytes_accessed=8 * 2**20, transcendentals=5504 * 4096),
    )(
        points, right_sides, skel_dev, proj_dev[0], skel_sel[0], proj_up[0], fetch_leaf,
        pair_target[0], pair_source[0], pair_count, far_use,
    )


def solution(mesh):
    in_specs = (
        P(None, "leaf"),
        P("rep", "leaf"),
        P("leaf", None),
        P("leaf", None, None),
        P("leaf", None, None),
        P("leaf", None, None, None),
        P("leaf", None),
        P("leaf", "rep", None),
        P("leaf", "rep", None),
        P("leaf", "rep"),
        P(None, "leaf"),
    )
    out_specs = P("rep", "leaf")
    return jax.shard_map(shards, mesh=mesh, in_specs=in_specs, out_specs=out_specs, check_vma=False)
```

```python
import jax
import jax.numpy as jnp
from jax import lax
from jax.experimental import pallas as pl
from jax.experimental.pallas import tpu as pltpu
from jax.sharding import PartitionSpec as P

MESH = pl.DeviceIdType.MESH
bf16, f32, i32 = jnp.bfloat16, jnp.float32, jnp.int32

kernel_scale = 3.0
to_log2 = 2.0 * kernel_scale * 1.4426950408889634
dead_bias = -16384.0

coords, width = 300, 384
leaves, leaf_len, groups, part = 16, 256, 4, 64
ring, cluster, levels = 8, 8, 6
rows_k = cluster * part
pieces, piece = 4, 4
tile = 2048
tiles = 2
mask_lane = 48

SCRATCH = dict(
    tgt=pltpu.VMEM((width, 4096), bf16),
    src3=pltpu.VMEM((128, 4096), bf16),
    acc=pltpu.VMEM((groups, 16, 4096), f32),
    proj=pltpu.VMEM((256, 4096), bf16),
    up=pltpu.VMEM((5, 256, 512), bf16),
    rpack=pltpu.VMEM((groups, 16, 1024), bf16),
    rq=pltpu.VMEM((groups, 16, 1024), bf16),
    lists=pltpu.VMEM((2, 256), i32),
    far_rows=pltpu.VMEM((8, 128), i32),
    masks=pltpu.VMEM((groups, 96, 128), bf16),
    bias=pltpu.VMEM((96, 128), f32),
    wq=pltpu.VMEM((groups, 16, 256), bf16),
    wmine=pltpu.VMEM((16, 256), bf16),
    picked=pltpu.VMEM((width, 256), f32),
    node=pltpu.VMEM((levels, groups, part, width), bf16),
    sib=pltpu.VMEM((levels - 1, groups, part, width), bf16),
    far=pltpu.VMEM((levels, part, width), bf16),
    want0=pltpu.VMEM((cluster, 1, 128), i32),
    want1=pltpu.VMEM((cluster, 1, 128), i32),
    want2=pltpu.VMEM((cluster, 1, 128), i32),
    want6=pltpu.VMEM((cluster, 1, 128), i32),
    want7=pltpu.VMEM((cluster, 1, 128), i32),
    want_s=pltpu.SMEM((5, cluster, 1, 128), i32),
    set0=pltpu.VMEM((leaves, part, width), bf16),
    set1=pltpu.VMEM((leaves, part, width), bf16),
    set2=pltpu.VMEM((leaves, part, width), bf16),
    set6=pltpu.VMEM((leaves, part, width), bf16),
    set7=pltpu.VMEM((leaves, part, width), bf16),
    pick=pltpu.VMEM((5, cluster, part, width), bf16),
    relay_out=pltpu.VMEM((2, 12, part, width), bf16),
    relay_in=pltpu.VMEM((2, 12, part, width), bf16),
    opposite=pltpu.VMEM((4, 2, part, width), bf16),
    pool=pltpu.VMEM((ring, cluster, part, width), bf16),
    stage=pltpu.VMEM((2, rows_k, width), bf16),
    weights=pltpu.VMEM((2, 64, rows_k), bf16),
    sum_out=pltpu.VMEM((3, tiles, 16, tile), bf16),
    sum_in=pltpu.VMEM((3, tiles, 16, tile), bf16),
    rq_s=pltpu.SemaphoreType.DMA((3,)),
    rq_r=pltpu.SemaphoreType.DMA((3,)),
    mask_s=pltpu.SemaphoreType.DMA((3,)),
    mask_r=pltpu.SemaphoreType.DMA((3,)),
    w_s=pltpu.SemaphoreType.DMA((3,)),
    w_r=pltpu.SemaphoreType.DMA((3,)),
    want_snd=pltpu.SemaphoreType.DMA((7,)),
    want_rcv=pltpu.SemaphoreType.DMA((7,)),
    table_s=pltpu.SemaphoreType.DMA((2, 2)),
    table_r=pltpu.SemaphoreType.DMA((2, 2)),
    early_s=pltpu.SemaphoreType.DMA((2,)),
    early_r=pltpu.SemaphoreType.DMA((2,)),
    first_s=pltpu.SemaphoreType.DMA((2, pieces)),
    first_r=pltpu.SemaphoreType.DMA((2, pieces)),
    second_s=pltpu.SemaphoreType.DMA((2, pieces)),
    second_r=pltpu.SemaphoreType.DMA((2, pieces)),
    third_s=pltpu.SemaphoreType.DMA((2, 3)),
    third_r=pltpu.SemaphoreType.DMA((2, 3)),
    fourth_s=pltpu.SemaphoreType.DMA((2,)),
    fourth_r=pltpu.SemaphoreType.DMA((2,)),
    spread_s=pltpu.SemaphoreType.DMA((ring, 7)),
    spread_r=pltpu.SemaphoreType.DMA((ring, 7)),
    level_s=pltpu.SemaphoreType.DMA((levels,)),
    level_r=pltpu.SemaphoreType.DMA((levels,)),
    sib_s=pltpu.SemaphoreType.DMA((levels - 1, 3)),
    sib_r=pltpu.SemaphoreType.DMA((levels - 1, 3)),
    sum_s=pltpu.SemaphoreType.DMA((3, tiles)),
    sum_r=pltpu.SemaphoreType.DMA((3, tiles)),
    local=pltpu.SemaphoreType.DMA((8,)),
)
INPUTS = (
    "points", "rights", "skel", "proj_hbm", "sel", "up_hbm", "fetch", "ptarget", "psource", "pcount", "far_use",
)


def iota(shape, dim):
    return lax.broadcasted_iota(i32, shape, dim)


def dot(a, b, dims=((1,), (0,))):
    return lax.dot_general(a, b, (dims, ((), ())), preferred_element_type=f32)


class Refs:
    pass


def kernel(*args):
    r = Refs()
    for name, ref in zip(INPUTS + ("out",) + tuple(SCRATCH), args):
        setattr(r, name, ref)
    me = lax.axis_index("leaf")
    y = lax.axis_index("rep")
    z, q = me // cluster, me % cluster

    def z_peer(step):
        return {"leaf": (z + step + ring) % ring * cluster + q}

    def q_peer(o):
        return {"leaf": z * cluster + (q + o) % cluster}

    def y_peer(o):
        return {"rep": (y + o) % groups}

    def level_peer(bit):
        low = (me >> bit) % 2
        return {"leaf": me + (1 - 2 * low) * 2**bit}

    def send(src, dst, s_sem, r_sem, peer):
        return pltpu.make_async_remote_copy(
            src_ref=src, dst_ref=dst, send_sem=s_sem, recv_sem=r_sem, device_id=peer, device_id_type=MESH
        )

    barrier = pltpu.get_barrier_semaphore()

    def greet(peer):
        pl.semaphore_signal(barrier, inc=1, device_id=peer, device_id_type=MESH)

    for o in range(1, 4):
        greet(y_peer(o))
    for o in range(1, 8):
        greet(q_peer(o))
    greet(z_peer(1))
    greet(z_peer(-1))
    greet(level_peer(4))
    greet(level_peer(5))

    proj_copy = pltpu.make_async_copy(r.proj_hbm, r.proj, r.local.at[0])
    up_copy = pltpu.make_async_copy(r.up_hbm, r.up, r.local.at[1])
    proj_copy.start()
    up_copy.start()

    stacked = jnp.concatenate([r.rights[:, k * 512 : (k + 1) * 512] for k in range(8)], axis=0)
    b_col = iota((512, 512), 1)
    from_col = (b_col >> 6) % 2 * 256 + (b_col >> 7) * 64 + b_col % 64
    order = (iota((512, 512), 0) == from_col).astype(bf16)
    packed = dot(stacked, order).astype(bf16)
    for k in range(8):
        for other in range(groups):
            r.rpack[other, :, k * 128 : (k + 1) * 128] = packed[
                k * 16 : (k + 1) * 16, other * 128 : (other + 1) * 128
            ]

    r.lists[...] = jnp.full((2, 256), -1, i32)
    r.lists[0:1, 0:192] = r.ptarget[...]
    r.lists[1:2, 0:192] = r.psource[...]
    live = iota((128, 256), 1) < r.pcount[...]
    hot_target = ((iota((128, 256), 0) - mask_lane == r.lists[0:1, :]) & live).astype(bf16)
    hot_source = (iota((96, 256), 0) == r.lists[1:2, :]).astype(bf16)
    r.masks[y] = dot(hot_source, hot_target, ((1,), (1,))).astype(bf16)
    r.want0[q] = jnp.full((1, 128), 0, i32)
    r.want0[q, :, 0:64] = r.fetch[...]

    @pl.loop(0, 8)
    def _(step):
        cols = pl.ds(pl.multiple_of(step * 512, 512), 512)
        r.tgt[0:288, cols] = r.points[0:288, cols]
        r.src3[0:32, cols] = r.points[256:288, cols]
        wide = r.points[:, cols].astype(f32)
        half = -0.5 * jnp.sum(wide * wide, axis=0, keepdims=True)
        high = half.astype(bf16).astype(f32)
        low = half - high
        r.tgt[288:304, cols] = jnp.zeros((16, 512), bf16)
        r.tgt[288:300, cols] = r.points[288:300, cols]
        tail = r.tgt[288:304, cols].astype(f32)
        row = iota((16, 512), 0)
        r.src3[32:48, cols] = jnp.where(
            row < 12, tail, jnp.where(row < 14, 1.0, jnp.where(row == 14, high, low))
        ).astype(bf16)
        r.tgt[288:304, cols] = jnp.where(
            row < 12, tail, jnp.where(row >= 14, 1.0, jnp.where(row == 12, high, low))
        ).astype(bf16)
        leaf_of = step * 2 + (iota((16, 512), 1) >> 8)
        r.tgt[304:320, cols] = (row == leaf_of).astype(bf16)
        r.tgt[320:384, cols] = jnp.zeros((64, 512), bf16)
        r.src3[48:128, cols] = jnp.zeros((80, 512), bf16)

    choose = (iota((part, 128), 1) == iota((part, 128), 0) + y % 2 * part).astype(bf16)
    unit = (iota((128, 128), 0) == iota((128, 128), 1)).astype(bf16)

    def quarter_cols(leaf):
        return pl.ds(pl.multiple_of(leaf * leaf_len + y // 2 * 128, 128), 128)

    @pl.loop(0, leaves)
    def _(leaf):
        r.set0[leaf, :, 0:256] = dot(choose, r.tgt[0:256, quarter_cols(leaf)], ((1,), (1,))).astype(bf16)

    def tables(hop, way):
        src = (r.want0, r.want1 if way == 0 else r.want7)[hop]
        dst = ((r.want1, r.want2), (r.want7, r.want6))[way][hop]
        return send(src, dst, r.table_s.at[hop, way], r.table_r.at[hop, way], z_peer(2 * way - 1))

    def early(way):
        dst = (r.set1, r.set7)[way]
        span = (slice(None), slice(None), pl.ds(0, 256))
        return send(r.set0.at[span], dst.at[span], r.early_s.at[way], r.early_r.at[way], z_peer(2 * way - 1))

    def first(way, n):
        span = (pl.ds(n * piece, piece), slice(None), pl.ds(256, 128))
        dst = (r.set1, r.set7)[way]
        return send(r.set0.at[span], dst.at[span], r.first_s.at[way, n], r.first_r.at[way, n], z_peer(2 * way - 1))

    def second(way, n):
        span = pl.ds(n * piece, piece)
        src, dst = ((r.set1, r.set2), (r.set7, r.set6))[way]
        return send(src.at[span], dst.at[span], r.second_s.at[way, n], r.second_r.at[way, n], z_peer(2 * way - 1))

    def third(way, n):
        span = pl.ds(n * 4, 4)
        return send(
            r.relay_out.at[way, span],
            r.relay_in.at[way, span],
            r.third_s.at[way, n],
            r.third_r.at[way, n],
            z_peer(2 * way - 1),
        )

    def fourth(way):
        return send(
            r.relay_in.at[way, pl.ds(0, 4)],
            r.opposite.at[:, 1 - way],
            r.fourth_s.at[way],
            r.fourth_r.at[way],
            z_peer(2 * way - 1),
        )

    pl.semaphore_wait(barrier, 14)

    for o in range(1, 4):
        dest = (y + o) % groups
        send(r.rpack.at[dest], r.rq.at[y], r.rq_s.at[o - 1], r.rq_r.at[o - 1], y_peer(o)).start()

    @pl.loop(1, 8)
    def _(o):
        send(r.want0.at[q], r.want0.at[q], r.want_snd.at[o - 1], r.want_rcv.at[o - 1], q_peer(o)).start()

    for o in range(1, 4):
        send(r.masks.at[y], r.masks.at[y], r.mask_s.at[o - 1], r.mask_r.at[o - 1], y_peer(o)).start()
    r.rq[y] = r.rpack[y]
    for way in range(2):
        early(way).start()

    proj_copy.wait()
    r.wmine[...] = dot(r.rights[...], r.proj[...], ((1,), (1,))).astype(bf16)
    r.wq[y] = r.wmine[...]
    for o in range(1, 4):
        send(r.wmine, r.wq.at[y], r.w_s.at[o - 1], r.w_r.at[o - 1], y_peer(o)).start()
    r.picked[...] = jnp.zeros((width, 256), f32)

    @pl.loop(0, 8)
    def _(step):
        cols = pl.ds(pl.multiple_of(step * 512, 512), 512)
        hot = (iota((512, 256), 0) + step * 512 == r.skel[...]).astype(bf16)
        r.picked[0:256] += dot(r.tgt[0:256, cols], hot)
        r.picked[256:384] += dot(r.src3[:, cols], hot)

    for o in range(1, 4):
        sender = (y - o + groups) % groups
        send(r.rpack.at[0], r.rq.at[sender], r.rq_s.at[o - 1], r.rq_r.at[o - 1], y_peer(o)).wait_recv()

    @pl.loop(0, leaves // 2)
    def _(pair):
        cols = pl.ds(pl.multiple_of(pair * 128, 128), 128)
        values = jnp.concatenate([jnp.zeros((64, 128), bf16), r.rq[:, :, cols].reshape(64, 128)], axis=0)
        turned = dot(unit, values, ((1,), (1,)))
        for odd in range(2):
            leaf = pair * 2 + odd
            own = dot(choose, r.src3[:, quarter_cols(leaf)], ((1,), (1,)))
            r.set0[leaf, :, 256:384] = (own + turned[odd * part : (odd + 1) * part]).astype(bf16)

    for n in range(pieces):
        for way in range(2):
            first(way, n).start()
    @pl.loop(1, 8)
    def _(o):
        sender = (q - o + cluster) % cluster
        send(r.want0.at[q], r.want0.at[sender], r.want_snd.at[o - 1], r.want_rcv.at[o - 1], q_peer(o)).wait_recv()

    for way in range(2):
        tables(0, way).start()

    def received(n):
        for way in range(2):
            if n == 0:
                early(way).wait_recv()
            first(way, n).wait_recv()

    def forward(n):
        for way in range(2):
            second(way, n).start()

    def to_scalars(slot, ref):
        copy = pltpu.make_async_copy(ref, r.want_s.at[slot], r.local.at[2 + slot])
        copy.start()
        copy.wait()

    to_scalars(0, r.want0)

    def spread_copy(k, o, src):
        return send(src, r.pool.at[k, q], r.spread_s.at[k, o - 1], r.spread_r.at[k, o - 1], q_peer(o))

    def spread_picked(k, slot, held):
        owner = (z + k) % ring * cluster + q

        @pl.loop(0, cluster)
        def _(t):
            r.pick[slot, t] = held[r.want_s[0, t, 0, owner]]

        @pl.loop(1, 8)
        def _(o):
            spread_copy(k, o, r.pick.at[slot, (q + o) % cluster]).start()

        r.pool[k, q] = r.pick[slot, q]

    def spread_relayed(k, way, half):
        @pl.loop(4 * half, 4 * half + 4)
        def _(t):
            @pl.when(t != q)
            def _():
                spread_copy(k, (t - q + cluster) % cluster, r.relay_in.at[way, 4 + t]).start()

            @pl.when(t == q)
            def _():
                r.pool[k, q] = r.relay_in[way, 4 + q]

    def spread_opposite():
        @pl.loop(1, 8)
        def _(o):
            t = (q + o) % cluster
            spread_copy(4, o, r.opposite.at[t // 2, t % 2]).start()

        r.pool[4, q] = r.opposite[q // 2, q % 2]

    def spread_arrived(k):
        @pl.loop(1, 8)
        def _(o):
            sender = (q - o + cluster) % cluster
            send(
                r.pick.at[0, 0], r.pool.at[k, sender], r.spread_s.at[k, o - 1], r.spread_r.at[k, o - 1], q_peer(o)
            ).wait_recv()

    spread_picked(0, 0, r.set0)

    for o in range(1, 4):
        sender = (y - o + groups) % groups
        send(r.wmine, r.wq.at[sender], r.w_s.at[o - 1], r.w_r.at[o - 1], y_peer(o)).wait_recv()
    lane = iota((256, 128), 1)
    w_turned = jnp.concatenate([jnp.zeros((64, 256), bf16), r.wq[...].reshape(64, 256)], axis=0)
    third_rows = r.picked[256:384].astype(bf16) + w_turned
    r.node[0, :, :, 0:256] = jnp.transpose(r.picked[0:256].astype(bf16)).reshape(groups, part, 256)
    r.node[0, :, :, 256:384] = jnp.transpose(third_rows).reshape(groups, part, 128)

    whole_levels = 1

    def level_copy(level):
        if level < whole_levels:
            src, dst = r.node.at[level], r.sib.at[level]
        else:
            src, dst = r.node.at[level, y], r.far.at[level]
        return send(src, dst, r.level_s.at[level], r.level_r.at[level], level_peer(level))

    def sib_copy(level, o, slot):
        return send(r.far.at[level], r.sib.at[level, slot], r.sib_s.at[level, o - 1], r.sib_r.at[level, o - 1], y_peer(o))

    def gather_sibling(level):
        level_copy(level).wait_recv()
        if level < whole_levels:
            r.far[level] = r.sib[level, y]
        elif level + 1 < levels:
            for o in range(1, 4):
                sib_copy(level, o, y).start()
            r.sib[level, y] = r.far[level]

    def climb(level):
        for o in range(1, 4 if level >= whole_levels else 1):
            sib_copy(level, o, (y - o + groups) % groups).wait_recv()
        upper = (me >> level) % 2
        own = r.node[level].reshape(256, width)
        other = r.sib[level].reshape(256, width)
        place = (r.sel[level] + 256 * upper) % 512
        hot = (iota((512, 256), 0) == place).astype(bf16)
        chosen = dot(hot[0:256], own, ((0,), (0,))) + dot(hot[256:512], other, ((0,), (0,)))
        own_cols = pl.ds(pl.multiple_of(upper * 256, 256), 256)
        other_cols = pl.ds(pl.multiple_of(256 - upper * 256, 256), 256)
        raised = dot(r.up[level, :, own_cols], own[:, 256:]) + dot(r.up[level, :, other_cols], other[:, 256:])
        r.node[level + 1, :, :, 0:256] = chosen[:, 0:256].astype(bf16).reshape(groups, part, 256)
        r.node[level + 1, :, :, 256:384] = (
            jnp.where(lane < 64, chosen[:, 256:], raised).astype(bf16).reshape(groups, part, 128)
        )
        level_copy(level + 1).start()

    level_copy(0).start()
    up_copy.wait()

    for o in range(1, 4):
        sender = (y - o + groups) % groups
        send(r.masks.at[y], r.masks.at[sender], r.mask_s.at[o - 1], r.mask_r.at[o - 1], y_peer(o)).wait_recv()
    pairs = sum(r.masks[g].astype(f32) for g in range(groups))
    lane96 = iota((96, 128), 1)
    in_mask = (lane96 >= mask_lane) & (lane96 < mask_lane + leaves)
    r.bias[...] = jnp.where(in_mask & (pairs < 0.5), dead_bias, 0.0)
    r.far_rows[...] = jnp.zeros((8, 128), i32)
    r.far_rows[0:6, 0:16] = r.far_use[...]
    used = pltpu.roll(r.far_rows[...], mask_lane, 1)
    r.bias[80:88] = jnp.where(in_mask[0:8] & (used == 0), dead_bias, 0.0)
    r.acc[...] = jnp.zeros((groups, 16, 4096), f32)

    def stage(ref, count, first_row, slot=0):
        rows = count * part
        r.stage[slot, 0:rows, 0:256] = ref[:, :, 0:256].reshape(rows, 256)
        bias = r.bias[pl.ds(first_row, 8), :][0:count]
        tail = (ref[:, :, 256:384].astype(f32) + bias[:, None, :]).astype(bf16).reshape(rows, 128)
        r.stage[slot, 0:rows, 256:384] = tail
        r.weights[slot, :, 0:rows] = jnp.transpose(tail)[64:128]

    def stage_near(k, slot=0):
        spread_arrived(k)
        stage(r.pool.at[k], cluster, pl.multiple_of(16 + (z + k) % ring * cluster, 8), slot)

    def stage_own(half):
        stage(r.set0.at[pl.ds(half * 8, 8)], 8, half * 8)

    def stage_far(slot=0):
        stage(r.far, levels, 80, slot)
        r.stage[slot, levels * part : rows_k, :] = jnp.zeros((rows_k - levels * part, width), bf16)
        r.weights[slot, :, levels * part : rows_k] = jnp.zeros((64, rows_k - levels * part), bf16)

    def tables_done():
        for way in range(2):
            tables(1, way).wait_recv()
        for slot, ref in ((1, r.want1), (2, r.want2), (3, r.want6), (4, r.want7)):
            to_scalars(slot, ref)

    def pass_tables():
        for way in range(2):
            tables(0, way).wait_recv()
            tables(1, way).start()

    def relay_wanted():
        for n in range(pieces):
            for way in range(2):
                second(way, n).wait_recv()
        for way in range(2):
            held = (r.set2, r.set6)[way]
            owner = (z + (2, 6)[way]) % ring * cluster + q
            near_table, far_table = ((4, 3), (1, 2))[way]

            @pl.loop(0, 4)
            def _(t):
                r.relay_out[way, t] = held[r.want_s[far_table, 2 * t + 1 - way, 0, owner]]

            third(way, 0).start()

            @pl.loop(0, cluster)
            def _(t):
                r.relay_out[way, 4 + t] = held[r.want_s[near_table, t, 0, owner]]

            third(way, 1).start()

    def relay_rest():
        for way in range(2):
            third(way, 2).start()

    def relay_opposite():
        for way in range(2):
            third(way, 0).wait_recv()
            fourth(way).start()

    def spread_third(half):
        for way in range(2):
            third(way, 1 + half).wait_recv()
        spread_relayed(3, 0, half)
        spread_relayed(5, 1, half)

    def spread_fourth():
        for way in range(2):
            fourth(way).wait_recv()
        spread_opposite()

    def sum_copy(o, index):
        return send(
            r.sum_out.at[o - 1, index],
            r.sum_in.at[o - 1, index],
            r.sum_s.at[o - 1, index],
            r.sum_r.at[o - 1, index],
            y_peer(o),
        )

    events = {
        0: [
            lambda: stage_own(0),
        ],
        1: [
            lambda: gather_sibling(0),
            lambda: climb(0),
            lambda: received(0),
            lambda: forward(0),
            pass_tables,
        ],
        2: [
            lambda: received(1),
            lambda: forward(1),
            lambda: stage_own(1),
        ],
        3: [
            lambda: gather_sibling(1),
            lambda: received(2),
            lambda: received(3),
            lambda: spread_picked(1, 1, r.set1),
            lambda: spread_picked(7, 2, r.set7),
        ],
        4: [
            lambda: climb(1),
            lambda: stage_near(0),
            tables_done,
        ],
        5: [
            lambda: gather_sibling(2),
        ],
        6: [
            lambda: climb(2),
            lambda: forward(2),
            lambda: forward(3),
            lambda: stage_near(1),
        ],
        7: [
            lambda: gather_sibling(3),
        ],
        8: [
            lambda: stage_near(7),
        ],
        9: [
            lambda: climb(3),
        ],
        10: [
            relay_wanted,
            lambda: spread_picked(2, 3, r.set2),
            lambda: spread_picked(6, 4, r.set6),
            lambda: gather_sibling(4),
            lambda: climb(4),
            relay_rest,
            relay_opposite,
            lambda: stage_near(2),
        ],
        11: [
            lambda: spread_third(0),
        ],
        12: [
            lambda: stage_near(6),
        ],
        13: [
            lambda: spread_third(1),
            lambda: gather_sibling(5),
        ],
        14: [
            stage_far,
        ],
        15: [
            spread_fourth,
        ],
        16: [
            lambda: stage_near(3),
        ],
        18: [
            lambda: stage_near(5),
        ],
        19: [
            lambda: stage_near(4, 1),
        ],
    }

    @pl.loop(0, 22)
    def _(step):
        for when, actions in events.items():

            @pl.when(step == when)
            def _(actions=actions):
                for act in actions:
                    act()

        final = step >= 18
        index = jnp.where(final, (step - 18) // 2, step % 2)
        slot = jnp.where(final, step % 2, 0)
        cols = pl.ds(pl.multiple_of(index * tile, tile), tile)
        exponent = dot(r.stage[slot], r.tgt[:, cols])
        values = jnp.exp2(exponent * to_log2).astype(bf16)
        r.acc[:, :, cols] += dot(r.weights[slot], values).reshape(groups, 16, tile)

        @pl.when(final & (step % 2 == 1))
        def _():
            for o in range(1, 4):
                r.sum_out[o - 1, index] = r.acc[(y + o) % groups, :, cols].astype(bf16)
                sum_copy(o, index).start()

    @pl.loop(0, tiles)
    def _(index):
        cols = pl.ds(pl.multiple_of(index * tile, tile), tile)
        total = r.acc[y, :, cols]
        for o in range(1, 4):
            sum_copy(o, index).wait_recv()
            total += r.sum_in[o - 1, index].astype(f32)
        r.out[:, cols] = total

    for o in range(1, 4):
        send(r.rpack.at[0], r.rq.at[y], r.rq_s.at[o - 1], r.rq_r.at[o - 1], y_peer(o)).wait_send()
        send(r.masks.at[y], r.masks.at[y], r.mask_s.at[o - 1], r.mask_r.at[o - 1], y_peer(o)).wait_send()
        send(r.wmine, r.wq.at[y], r.w_s.at[o - 1], r.w_r.at[o - 1], y_peer(o)).wait_send()
        for level in range(whole_levels, levels - 1):
            sib_copy(level, o, y).wait_send()
    for level in range(levels):
        level_copy(level).wait_send()
    for way in range(2):
        for hop in range(2):
            tables(hop, way).wait_send()
        early(way).wait_send()
        for n in range(pieces):
            first(way, n).wait_send()
            second(way, n).wait_send()
        for n in range(3):
            third(way, n).wait_send()
        fourth(way).wait_send()

    @pl.loop(1, 8)
    def _(o):
        send(r.want0.at[q], r.want0.at[q], r.want_snd.at[o - 1], r.want_rcv.at[o - 1], q_peer(o)).wait_send()
        for k in range(ring):
            spread_copy(k, o, r.pick.at[0, 0]).wait_send()

    @pl.loop(0, tiles)
    def _(index):
        for o in range(1, 4):
            sum_copy(o, index).wait_send()


def shards(
    points, right_sides, skel_dev, proj_dev, skel_sel, proj_up, fetch_leaf,
    pair_target, pair_source, pair_count, far_use,
):
    vmem = pl.BlockSpec(memory_space=pltpu.VMEM)
    anywhere = pl.BlockSpec(memory_space=pl.ANY)
    specs = [anywhere if name.endswith("hbm") else vmem for name in INPUTS]
    return pl.pallas_call(
        kernel,
        out_shape=jax.ShapeDtypeStruct((16, 4096), f32),
        in_specs=specs,
        out_specs=vmem,
        scratch_shapes=list(SCRATCH.values()),
        compiler_params=pltpu.CompilerParams(
            collective_id=0, has_side_effects=True, vmem_limit_bytes=60 * 2**20
        ),
        cost_estimate=pl.CostEstimate(flops=2 * 5504 * 4096 * 448, bytes_accessed=8 * 2**20, transcendentals=5504 * 4096),
    )(
        points, right_sides, skel_dev, proj_dev[0], jnp.transpose(skel_sel, (1, 0, 2)), proj_up[0], fetch_leaf,
        pair_target[0], pair_source[0], pair_count, far_use,
    )


def solution(mesh):
    in_specs = (
        P(None, "leaf"),
        P("rep", "leaf"),
        P("leaf", None),
        P("leaf", None, None),
        P("leaf", None, None),
        P("leaf", None, None, None),
        P("leaf", None),
        P("leaf", "rep", None),
        P("leaf", "rep", None),
        P("leaf", "rep"),
        P(None, "leaf"),
    )
    out_specs = P("rep", "leaf")
    return jax.shard_map(shards, mesh=mesh, in_specs=in_specs, out_specs=out_specs, check_vma=False)
```

```python
import jax
import jax.numpy as jnp
from jax import lax
from jax.experimental import pallas as pl
from jax.experimental.pallas import tpu as pltpu
from jax.sharding import PartitionSpec as P

MESH = pl.DeviceIdType.MESH
bf16, f32, i32 = jnp.bfloat16, jnp.float32, jnp.int32

kernel_scale = 3.0
to_log2 = 2.0 * kernel_scale * 1.4426950408889634
dead_bias = -16384.0

coords, width = 300, 384
leaves, leaf_len, groups, part = 16, 256, 4, 64
ring, cluster, levels = 8, 8, 6
rows_k = cluster * part
pieces, piece = 4, 4
tile = 2048
tiles = 2
mask_lane = 48

SCRATCH = dict(
    tgt=pltpu.VMEM((width, 4096), bf16),
    src3=pltpu.VMEM((128, 4096), bf16),
    acc=pltpu.VMEM((groups, 16, 4096), f32),
    proj=pltpu.VMEM((256, 4096), bf16),
    up=pltpu.VMEM((5, 256, 512), bf16),
    rpack=pltpu.VMEM((groups, 16, 1024), bf16),
    rq=pltpu.VMEM((groups, 16, 1024), bf16),
    lists=pltpu.VMEM((2, 256), i32),
    far_rows=pltpu.VMEM((8, 128), i32),
    masks=pltpu.VMEM((groups, 96, 128), bf16),
    bias=pltpu.VMEM((96, 128), f32),
    wq=pltpu.VMEM((groups, 16, 256), bf16),
    wmine=pltpu.VMEM((16, 256), bf16),
    picked=pltpu.VMEM((width, 256), f32),
    node=pltpu.VMEM((levels, groups, part, width), bf16),
    sib=pltpu.VMEM((levels - 1, groups, part, width), bf16),
    far=pltpu.VMEM((levels, part, width), bf16),
    want0=pltpu.VMEM((cluster, 1, 128), i32),
    want1=pltpu.VMEM((cluster, 1, 128), i32),
    want2=pltpu.VMEM((cluster, 1, 128), i32),
    want6=pltpu.VMEM((cluster, 1, 128), i32),
    want7=pltpu.VMEM((cluster, 1, 128), i32),
    want_s=pltpu.SMEM((5, cluster, 1, 128), i32),
    set0=pltpu.VMEM((leaves, part, width), bf16),
    set1=pltpu.VMEM((leaves, part, width), bf16),
    set2=pltpu.VMEM((leaves, part, width), bf16),
    set6=pltpu.VMEM((leaves, part, width), bf16),
    set7=pltpu.VMEM((leaves, part, width), bf16),
    pick=pltpu.VMEM((5, cluster, part, width), bf16),
    relay_out=pltpu.VMEM((2, 12, part, width), bf16),
    relay_in=pltpu.VMEM((2, 12, part, width), bf16),
    opposite=pltpu.VMEM((4, 2, part, width), bf16),
    pool=pltpu.VMEM((ring, cluster, part, width), bf16),
    stage=pltpu.VMEM((2, rows_k, width), bf16),
    weights=pltpu.VMEM((2, 64, rows_k), bf16),
    sum_out=pltpu.VMEM((3, tiles, 16, tile), bf16),
    sum_in=pltpu.VMEM((3, tiles, 16, tile), bf16),
    rq_s=pltpu.SemaphoreType.DMA((3,)),
    rq_r=pltpu.SemaphoreType.DMA((3,)),
    mask_s=pltpu.SemaphoreType.DMA((3,)),
    mask_r=pltpu.SemaphoreType.DMA((3,)),
    w_s=pltpu.SemaphoreType.DMA((3,)),
    w_r=pltpu.SemaphoreType.DMA((3,)),
    want_snd=pltpu.SemaphoreType.DMA((7,)),
    want_rcv=pltpu.SemaphoreType.DMA((7,)),
    table_s=pltpu.SemaphoreType.DMA((2, 2)),
    table_r=pltpu.SemaphoreType.DMA((2, 2)),
    early_s=pltpu.SemaphoreType.DMA((2,)),
    early_r=pltpu.SemaphoreType.DMA((2,)),
    first_s=pltpu.SemaphoreType.DMA((2, pieces)),
    first_r=pltpu.SemaphoreType.DMA((2, pieces)),
    second_s=pltpu.SemaphoreType.DMA((2, pieces)),
    second_r=pltpu.SemaphoreType.DMA((2, pieces)),
    third_s=pltpu.SemaphoreType.DMA((2, 3)),
    third_r=pltpu.SemaphoreType.DMA((2, 3)),
    fourth_s=pltpu.SemaphoreType.DMA((2,)),
    fourth_r=pltpu.SemaphoreType.DMA((2,)),
    spread_s=pltpu.SemaphoreType.DMA((ring, 7)),
    spread_r=pltpu.SemaphoreType.DMA((ring, 7)),
    level_s=pltpu.SemaphoreType.DMA((levels,)),
    level_r=pltpu.SemaphoreType.DMA((levels,)),
    sib_s=pltpu.SemaphoreType.DMA((levels - 1, 3)),
    sib_r=pltpu.SemaphoreType.DMA((levels - 1, 3)),
    sum_s=pltpu.SemaphoreType.DMA((3, tiles)),
    sum_r=pltpu.SemaphoreType.DMA((3, tiles)),
    local=pltpu.SemaphoreType.DMA((8,)),
)
INPUTS = (
    "points", "rights", "skel", "proj_hbm", "sel", "up_hbm", "fetch", "ptarget", "psource", "pcount", "far_use",
)


def iota(shape, dim):
    return lax.broadcasted_iota(i32, shape, dim)


def dot(a, b, dims=((1,), (0,))):
    return lax.dot_general(a, b, (dims, ((), ())), preferred_element_type=f32)


class Refs:
    pass


def kernel(*args):
    r = Refs()
    for name, ref in zip(INPUTS + ("out",) + tuple(SCRATCH), args):
        setattr(r, name, ref)
    me = lax.axis_index("leaf")
    y = lax.axis_index("rep")
    z, q = me // cluster, me % cluster

    def z_peer(step):
        return {"leaf": (z + step + ring) % ring * cluster + q}

    def q_peer(o):
        return {"leaf": z * cluster + (q + o) % cluster}

    def y_peer(o):
        return {"rep": (y + o) % groups}

    def level_peer(bit):
        low = (me >> bit) % 2
        return {"leaf": me + (1 - 2 * low) * 2**bit}

    def send(src, dst, s_sem, r_sem, peer):
        return pltpu.make_async_remote_copy(
            src_ref=src, dst_ref=dst, send_sem=s_sem, recv_sem=r_sem, device_id=peer, device_id_type=MESH
        )

    barrier = pltpu.get_barrier_semaphore()

    def greet(peer):
        pl.semaphore_signal(barrier, inc=1, device_id=peer, device_id_type=MESH)

    for o in range(1, 4):
        greet(y_peer(o))
    for o in range(1, 8):
        greet(q_peer(o))
    greet(z_peer(1))
    greet(z_peer(-1))
    greet(level_peer(4))
    greet(level_peer(5))

    proj_copy = pltpu.make_async_copy(r.proj_hbm, r.proj, r.local.at[0])
    up_copy = pltpu.make_async_copy(r.up_hbm, r.up, r.local.at[1])
    proj_copy.start()
    up_copy.start()

    stacked = jnp.concatenate([r.rights[:, k * 512 : (k + 1) * 512] for k in range(8)], axis=0)
    b_col = iota((512, 512), 1)
    from_col = (b_col >> 6) % 2 * 256 + (b_col >> 7) * 64 + b_col % 64
    order = (iota((512, 512), 0) == from_col).astype(bf16)
    packed = dot(stacked, order).astype(bf16)
    for k in range(8):
        for other in range(groups):
            r.rpack[other, :, k * 128 : (k + 1) * 128] = packed[
                k * 16 : (k + 1) * 16, other * 128 : (other + 1) * 128
            ]

    r.lists[...] = jnp.full((2, 256), -1, i32)
    r.lists[0:1, 0:192] = r.ptarget[...]
    r.lists[1:2, 0:192] = r.psource[...]
    live = iota((128, 256), 1) < r.pcount[...]
    hot_target = ((iota((128, 256), 0) - mask_lane == r.lists[0:1, :]) & live).astype(bf16)
    hot_source = (iota((96, 256), 0) == r.lists[1:2, :]).astype(bf16)
    r.masks[y] = dot(hot_source, hot_target, ((1,), (1,))).astype(bf16)
    r.want0[q] = jnp.full((1, 128), 0, i32)
    r.want0[q, :, 0:64] = r.fetch[...]

    @pl.loop(0, 8)
    def _(step):
        cols = pl.ds(pl.multiple_of(step * 512, 512), 512)
        r.tgt[0:288, cols] = r.points[0:288, cols]
        r.src3[0:32, cols] = r.points[256:288, cols]
        wide = r.points[:, cols].astype(f32)
        half = -0.5 * jnp.sum(wide * wide, axis=0, keepdims=True)
        high = half.astype(bf16).astype(f32)
        low = half - high
        r.tgt[288:304, cols] = jnp.zeros((16, 512), bf16)
        r.tgt[288:300, cols] = r.points[288:300, cols]
        tail = r.tgt[288:304, cols].astype(f32)
        row = iota((16, 512), 0)
        r.src3[32:48, cols] = jnp.where(
            row < 12, tail, jnp.where(row < 14, 1.0, jnp.where(row == 14, high, low))
        ).astype(bf16)
        r.tgt[288:304, cols] = jnp.where(
            row < 12, tail, jnp.where(row >= 14, 1.0, jnp.where(row == 12, high, low))
        ).astype(bf16)
        leaf_of = step * 2 + (iota((16, 512), 1) >> 8)
        r.tgt[304:320, cols] = (row == leaf_of).astype(bf16)
        r.tgt[320:384, cols] = jnp.zeros((64, 512), bf16)
        r.src3[48:128, cols] = jnp.zeros((80, 512), bf16)

    choose = (iota((part, 128), 1) == iota((part, 128), 0) + y % 2 * part).astype(bf16)
    unit = (iota((128, 128), 0) == iota((128, 128), 1)).astype(bf16)

    def quarter_cols(leaf):
        return pl.ds(pl.multiple_of(leaf * leaf_len + y // 2 * 128, 128), 128)

    @pl.loop(0, leaves)
    def _(leaf):
        r.set0[leaf, :, 0:256] = dot(choose, r.tgt[0:256, quarter_cols(leaf)], ((1,), (1,))).astype(bf16)

    def tables(hop, way):
        src = (r.want0, r.want1 if way == 0 else r.want7)[hop]
        dst = ((r.want1, r.want2), (r.want7, r.want6))[way][hop]
        return send(src, dst, r.table_s.at[hop, way], r.table_r.at[hop, way], z_peer(2 * way - 1))

    def early(way):
        dst = (r.set1, r.set7)[way]
        span = (slice(None), slice(None), pl.ds(0, 256))
        return send(r.set0.at[span], dst.at[span], r.early_s.at[way], r.early_r.at[way], z_peer(2 * way - 1))

    def first(way, n):
        span = (pl.ds(n * piece, piece), slice(None), pl.ds(256, 128))
        dst = (r.set1, r.set7)[way]
        return send(r.set0.at[span], dst.at[span], r.first_s.at[way, n], r.first_r.at[way, n], z_peer(2 * way - 1))

    def second(way, n):
        span = pl.ds(n * piece, piece)
        src, dst = ((r.set1, r.set2), (r.set7, r.set6))[way]
        return send(src.at[span], dst.at[span], r.second_s.at[way, n], r.second_r.at[way, n], z_peer(2 * way - 1))

    def third(way, n):
        span = pl.ds(n * 4, 4)
        return send(
            r.relay_out.at[way, span],
            r.relay_in.at[way, span],
            r.third_s.at[way, n],
            r.third_r.at[way, n],
            z_peer(2 * way - 1),
        )

    def fourth(way):
        return send(
            r.relay_in.at[way, pl.ds(0, 4)],
            r.opposite.at[:, 1 - way],
            r.fourth_s.at[way],
            r.fourth_r.at[way],
            z_peer(2 * way - 1),
        )

    pl.semaphore_wait(barrier, 14)

    for o in range(1, 4):
        dest = (y + o) % groups
        send(r.rpack.at[dest], r.rq.at[y], r.rq_s.at[o - 1], r.rq_r.at[o - 1], y_peer(o)).start()

    @pl.loop(1, 8)
    def _(o):
        send(r.want0.at[q], r.want0.at[q], r.want_snd.at[o - 1], r.want_rcv.at[o - 1], q_peer(o)).start()

    for o in range(1, 4):
        send(r.masks.at[y], r.masks.at[y], r.mask_s.at[o - 1], r.mask_r.at[o - 1], y_peer(o)).start()
    r.rq[y] = r.rpack[y]
    for way in range(2):
        early(way).start()

    proj_copy.wait()
    r.wmine[...] = dot(r.rights[...], r.proj[...], ((1,), (1,))).astype(bf16)
    r.wq[y] = r.wmine[...]
    for o in range(1, 4):
        send(r.wmine, r.wq.at[y], r.w_s.at[o - 1], r.w_r.at[o - 1], y_peer(o)).start()
    r.picked[...] = jnp.zeros((width, 256), f32)

    @pl.loop(0, 8)
    def _(step):
        cols = pl.ds(pl.multiple_of(step * 512, 512), 512)
        hot = (iota((512, 256), 0) + step * 512 == r.skel[...]).astype(bf16)
        r.picked[0:256] += dot(r.tgt[0:256, cols], hot)
        r.picked[256:384] += dot(r.src3[:, cols], hot)

    for o in range(1, 4):
        sender = (y - o + groups) % groups
        send(r.rpack.at[0], r.rq.at[sender], r.rq_s.at[o - 1], r.rq_r.at[o - 1], y_peer(o)).wait_recv()

    @pl.loop(0, leaves // 2)
    def _(pair):
        cols = pl.ds(pl.multiple_of(pair * 128, 128), 128)
        values = jnp.concatenate([jnp.zeros((64, 128), bf16), r.rq[:, :, cols].reshape(64, 128)], axis=0)
        turned = dot(unit, values, ((1,), (1,)))
        for odd in range(2):
            leaf = pair * 2 + odd
            own = dot(choose, r.src3[:, quarter_cols(leaf)], ((1,), (1,)))
            r.set0[leaf, :, 256:384] = (own + turned[odd * part : (odd + 1) * part]).astype(bf16)

    for n in range(pieces):
        for way in range(2):
            first(way, n).start()
    @pl.loop(1, 8)
    def _(o):
        sender = (q - o + cluster) % cluster
        send(r.want0.at[q], r.want0.at[sender], r.want_snd.at[o - 1], r.want_rcv.at[o - 1], q_peer(o)).wait_recv()

    for way in range(2):
        tables(0, way).start()

    def received(n):
        for way in range(2):
            if n == 0:
                early(way).wait_recv()
            first(way, n).wait_recv()

    def forward(n):
        for way in range(2):
            second(way, n).start()

    def to_scalars(slot, ref):
        copy = pltpu.make_async_copy(ref, r.want_s.at[slot], r.local.at[2 + slot])
        copy.start()
        copy.wait()

    to_scalars(0, r.want0)

    def spread_copy(k, o, src):
        return send(src, r.pool.at[k, q], r.spread_s.at[k, o - 1], r.spread_r.at[k, o - 1], q_peer(o))

    def spread_picked(k, slot, held):
        owner = (z + k) % ring * cluster + q

        @pl.loop(0, cluster)
        def _(t):
            r.pick[slot, t] = held[r.want_s[0, t, 0, owner]]

        @pl.loop(1, 8)
        def _(o):
            spread_copy(k, o, r.pick.at[slot, (q + o) % cluster]).start()

        r.pool[k, q] = r.pick[slot, q]

    def spread_relayed(k, way, half):
        @pl.loop(4 * half, 4 * half + 4)
        def _(t):
            @pl.when(t != q)
            def _():
                spread_copy(k, (t - q + cluster) % cluster, r.relay_in.at[way, 4 + t]).start()

            @pl.when(t == q)
            def _():
                r.pool[k, q] = r.relay_in[way, 4 + q]

    def spread_opposite():
        @pl.loop(1, 8)
        def _(o):
            t = (q + o) % cluster
            spread_copy(4, o, r.opposite.at[t // 2, t % 2]).start()

        r.pool[4, q] = r.opposite[q // 2, q % 2]

    def spread_arrived(k):
        @pl.loop(1, 8)
        def _(o):
            sender = (q - o + cluster) % cluster
            send(
                r.pick.at[0, 0], r.pool.at[k, sender], r.spread_s.at[k, o - 1], r.spread_r.at[k, o - 1], q_peer(o)
            ).wait_recv()


    for o in range(1, 4):
        sender = (y - o + groups) % groups
        send(r.wmine, r.wq.at[sender], r.w_s.at[o - 1], r.w_r.at[o - 1], y_peer(o)).wait_recv()
    lane = iota((256, 128), 1)
    w_turned = jnp.concatenate([jnp.zeros((64, 256), bf16), r.wq[...].reshape(64, 256)], axis=0)
    third_rows = r.picked[256:384].astype(bf16) + w_turned
    r.node[0, :, :, 0:256] = jnp.transpose(r.picked[0:256].astype(bf16)).reshape(groups, part, 256)
    r.node[0, :, :, 256:384] = jnp.transpose(third_rows).reshape(groups, part, 128)

    whole_levels = 1

    def level_copy(level):
        if level < whole_levels:
            src, dst = r.node.at[level], r.sib.at[level]
        else:
            src, dst = r.node.at[level, y], r.far.at[level]
        return send(src, dst, r.level_s.at[level], r.level_r.at[level], level_peer(level))

    def sib_copy(level, o, slot):
        return send(r.far.at[level], r.sib.at[level, slot], r.sib_s.at[level, o - 1], r.sib_r.at[level, o - 1], y_peer(o))

    def gather_sibling(level):
        level_copy(level).wait_recv()
        if level < whole_levels:
            r.far[level] = r.sib[level, y]
        elif level + 1 < levels:
            for o in (2, 1, 3):
                sib_copy(level, o, y).start()
            r.sib[level, y] = r.far[level]

    def climb(level):
        for o in range(1, 4 if level >= whole_levels else 1):
            sib_copy(level, o, (y - o + groups) % groups).wait_recv()
        upper = (me >> level) % 2
        own = r.node[level].reshape(256, width)
        other = r.sib[level].reshape(256, width)
        place = (r.sel[level] + 256 * upper) % 512
        hot = (iota((512, 256), 0) == place).astype(bf16)
        chosen = dot(hot[0:256], own, ((0,), (0,))) + dot(hot[256:512], other, ((0,), (0,)))
        own_cols = pl.ds(pl.multiple_of(upper * 256, 256), 256)
        other_cols = pl.ds(pl.multiple_of(256 - upper * 256, 256), 256)
        raised = dot(r.up[level, :, own_cols], own[:, 256:]) + dot(r.up[level, :, other_cols], other[:, 256:])
        r.node[level + 1, :, :, 0:256] = chosen[:, 0:256].astype(bf16).reshape(groups, part, 256)
        r.node[level + 1, :, :, 256:384] = (
            jnp.where(lane < 64, chosen[:, 256:], raised).astype(bf16).reshape(groups, part, 128)
        )
        level_copy(level + 1).start()

    level_copy(0).start()
    spread_picked(0, 0, r.set0)
    up_copy.wait()

    for o in range(1, 4):
        sender = (y - o + groups) % groups
        send(r.masks.at[y], r.masks.at[sender], r.mask_s.at[o - 1], r.mask_r.at[o - 1], y_peer(o)).wait_recv()
    pairs = sum(r.masks[g].astype(f32) for g in range(groups))
    lane96 = iota((96, 128), 1)
    in_mask = (lane96 >= mask_lane) & (lane96 < mask_lane + leaves)
    r.bias[...] = jnp.where(in_mask & (pairs < 0.5), dead_bias, 0.0)
    r.far_rows[...] = jnp.zeros((8, 128), i32)
    r.far_rows[0:6, 0:16] = r.far_use[...]
    used = pltpu.roll(r.far_rows[...], mask_lane, 1)
    r.bias[80:88] = jnp.where(in_mask[0:8] & (used == 0), dead_bias, 0.0)
    r.acc[...] = jnp.zeros((groups, 16, 4096), f32)

    def stage(ref, count, first_row, slot=0):
        rows = count * part
        r.stage[slot, 0:rows, 0:256] = ref[:, :, 0:256].reshape(rows, 256)
        bias = r.bias[pl.ds(first_row, 8), :][0:count]
        tail = (ref[:, :, 256:384].astype(f32) + bias[:, None, :]).astype(bf16).reshape(rows, 128)
        r.stage[slot, 0:rows, 256:384] = tail
        r.weights[slot, :, 0:rows] = jnp.transpose(tail)[64:128]

    def stage_near(k, slot=0):
        spread_arrived(k)
        stage(r.pool.at[k], cluster, pl.multiple_of(16 + (z + k) % ring * cluster, 8), slot)

    def stage_own(half):
        stage(r.set0.at[pl.ds(half * 8, 8)], 8, half * 8)

    def stage_far(slot=0):
        stage(r.far, levels, 80, slot)
        r.stage[slot, levels * part : rows_k, :] = jnp.zeros((rows_k - levels * part, width), bf16)
        r.weights[slot, :, levels * part : rows_k] = jnp.zeros((64, rows_k - levels * part), bf16)

    def tables_done():
        for way in range(2):
            tables(1, way).wait_recv()
        for slot, ref in ((1, r.want1), (2, r.want2), (3, r.want6), (4, r.want7)):
            to_scalars(slot, ref)

    def pass_tables():
        for way in range(2):
            tables(0, way).wait_recv()
            tables(1, way).start()

    def relay_wanted():
        for n in range(pieces):
            for way in range(2):
                second(way, n).wait_recv()
        for way in range(2):
            held = (r.set2, r.set6)[way]
            owner = (z + (2, 6)[way]) % ring * cluster + q
            near_table, far_table = ((4, 3), (1, 2))[way]

            @pl.loop(0, 4)
            def _(t):
                r.relay_out[way, t] = held[r.want_s[far_table, 2 * t + 1 - way, 0, owner]]

            third(way, 0).start()

            @pl.loop(0, cluster)
            def _(t):
                r.relay_out[way, 4 + t] = held[r.want_s[near_table, t, 0, owner]]

            third(way, 1).start()

    def relay_rest():
        for way in range(2):
            third(way, 2).start()

    def relay_opposite():
        for way in range(2):
            third(way, 0).wait_recv()
            fourth(way).start()

    def spread_third(half):
        for way in range(2):
            third(way, 1 + half).wait_recv()
        spread_relayed(3, 0, half)
        spread_relayed(5, 1, half)

    def spread_fourth():
        for way in range(2):
            fourth(way).wait_recv()
        spread_opposite()

    def sum_copy(o, index):
        return send(
            r.sum_out.at[o - 1, index],
            r.sum_in.at[o - 1, index],
            r.sum_s.at[o - 1, index],
            r.sum_r.at[o - 1, index],
            y_peer(o),
        )

    events = {
        0: [
            lambda: stage_own(0),
        ],
        1: [
            lambda: gather_sibling(0),
            lambda: climb(0),
            lambda: received(0),
            lambda: forward(0),
            pass_tables,
        ],
        2: [
            lambda: received(1),
            lambda: forward(1),
            lambda: stage_own(1),
        ],
        3: [
            lambda: gather_sibling(1),
            lambda: received(2),
            lambda: received(3),
            lambda: spread_picked(1, 1, r.set1),
            lambda: spread_picked(7, 2, r.set7),
        ],
        4: [
            lambda: climb(1),
            lambda: stage_near(0),
            tables_done,
        ],
        5: [
            lambda: gather_sibling(2),
        ],
        6: [
            lambda: climb(2),
            lambda: forward(2),
            lambda: forward(3),
            lambda: stage_near(1),
        ],
        7: [
            lambda: gather_sibling(3),
        ],
        8: [
            lambda: stage_near(7),
        ],
        9: [
            lambda: climb(3),
        ],
        10: [
            relay_wanted,
            lambda: spread_picked(2, 3, r.set2),
            lambda: spread_picked(6, 4, r.set6),
            lambda: gather_sibling(4),
            lambda: climb(4),
            relay_rest,
            relay_opposite,
            lambda: stage_near(2),
        ],
        11: [
            lambda: spread_third(0),
        ],
        12: [
            lambda: stage_near(6),
        ],
        13: [
            lambda: spread_third(1),
            lambda: gather_sibling(5),
        ],
        14: [
            stage_far,
        ],
        15: [
            spread_fourth,
        ],
        16: [
            lambda: stage_near(3),
        ],
        18: [
            lambda: stage_near(5),
        ],
        19: [
            lambda: stage_near(4, 1),
        ],
    }

    @pl.loop(0, 22)
    def _(step):
        for when, actions in events.items():

            @pl.when(step == when)
            def _(actions=actions):
                for act in actions:
                    act()

        final = step >= 18
        index = jnp.where(final, (step - 18) // 2, step % 2)
        slot = jnp.where(final, step % 2, 0)
        cols = pl.ds(pl.multiple_of(index * tile, tile), tile)
        exponent = dot(r.stage[slot], r.tgt[:, cols])
        values = jnp.exp2(exponent * to_log2).astype(bf16)
        r.acc[:, :, cols] += dot(r.weights[slot], values).reshape(groups, 16, tile)

        @pl.when(final & (step % 2 == 1))
        def _():
            for o in (2, 1, 3):
                r.sum_out[o - 1, index] = r.acc[(y + o) % groups, :, cols].astype(bf16)
                sum_copy(o, index).start()

    @pl.loop(0, tiles)
    def _(index):
        cols = pl.ds(pl.multiple_of(index * tile, tile), tile)
        total = r.acc[y, :, cols]
        for o in range(1, 4):
            sum_copy(o, index).wait_recv()
            total += r.sum_in[o - 1, index].astype(f32)
        r.out[:, cols] = total

    for o in range(1, 4):
        send(r.rpack.at[0], r.rq.at[y], r.rq_s.at[o - 1], r.rq_r.at[o - 1], y_peer(o)).wait_send()
        send(r.masks.at[y], r.masks.at[y], r.mask_s.at[o - 1], r.mask_r.at[o - 1], y_peer(o)).wait_send()
        send(r.wmine, r.wq.at[y], r.w_s.at[o - 1], r.w_r.at[o - 1], y_peer(o)).wait_send()
        for level in range(whole_levels, levels - 1):
            sib_copy(level, o, y).wait_send()
    for level in range(levels):
        level_copy(level).wait_send()
    for way in range(2):
        for hop in range(2):
            tables(hop, way).wait_send()
        early(way).wait_send()
        for n in range(pieces):
            first(way, n).wait_send()
            second(way, n).wait_send()
        for n in range(3):
            third(way, n).wait_send()
        fourth(way).wait_send()

    @pl.loop(1, 8)
    def _(o):
        send(r.want0.at[q], r.want0.at[q], r.want_snd.at[o - 1], r.want_rcv.at[o - 1], q_peer(o)).wait_send()
        for k in range(ring):
            spread_copy(k, o, r.pick.at[0, 0]).wait_send()

    @pl.loop(0, tiles)
    def _(index):
        for o in range(1, 4):
            sum_copy(o, index).wait_send()


def shards(
    points, right_sides, skel_dev, proj_dev, skel_sel, proj_up, fetch_leaf,
    pair_target, pair_source, pair_count, far_use,
):
    vmem = pl.BlockSpec(memory_space=pltpu.VMEM)
    anywhere = pl.BlockSpec(memory_space=pl.ANY)
    specs = [anywhere if name.endswith("hbm") else vmem for name in INPUTS]
    return pl.pallas_call(
        kernel,
        out_shape=jax.ShapeDtypeStruct((16, 4096), f32),
        in_specs=specs,
        out_specs=vmem,
        scratch_shapes=list(SCRATCH.values()),
        compiler_params=pltpu.CompilerParams(
            collective_id=0, has_side_effects=True, vmem_limit_bytes=60 * 2**20
        ),
        cost_estimate=pl.CostEstimate(flops=2 * 5504 * 4096 * 448, bytes_accessed=8 * 2**20, transcendentals=5504 * 4096),
    )(
        points, right_sides, skel_dev, proj_dev[0], jnp.transpose(skel_sel, (1, 0, 2)), proj_up[0], fetch_leaf,
        pair_target[0], pair_source[0], pair_count, far_use,
    )


def solution(mesh):
    in_specs = (
        P(None, "leaf"),
        P("rep", "leaf"),
        P("leaf", None),
        P("leaf", None, None),
        P("leaf", None, None),
        P("leaf", None, None, None),
        P("leaf", None),
        P("leaf", "rep", None),
        P("leaf", "rep", None),
        P("leaf", "rep"),
        P(None, "leaf"),
    )
    out_specs = P("rep", "leaf")
    return jax.shard_map(shards, mesh=mesh, in_specs=in_specs, out_specs=out_specs, check_vma=False)
```
